128 devices in a mesh: row: 8 (over y, z_lo), col: 16 (over x, z_hi, core).
Axes of the slice: x: 4, y: 4, z: 4 (z_hi: 2, z_lo: 2; z = z_hi * 2 + z_lo), core: 2. Of those that a mesh axis runs over, the one named last changes fastest.
Arguments:
- picture_embedding_matrix: bfloat16 [20480, 1152], P(('row', 'col')), may hold values from -0.1875 to 0.1875
- caption_embedding_matrix: bfloat16 [20480, 1152], P(('row', 'col')), may hold values from -0.1875 to 0.1875
- matching_caption_indices: int32 [20480], P(('row', 'col')), may hold values from 0 to 20479, each once
- sharpness_factor: float32 [1], replicated, may hold values from 5 to 20
- additive_shift_term: float32 [1], replicated, may hold values from -4 to -1
Outputs:
- image_grad: float32 [20480, 1152], P(('row', 'col'))
- text_grad: float32 [20480, 1152], P(('row', 'col'))
The draws below stay inside these ranges and needn't reach their ends.
Inputs may be any that keep to these rules, and one draw needn't show every extreme that they name: `matching_caption_indices`: it is a permutation: every text row is the positive of exactly one image row.
All inputs are finite; a program needn't handle non-finite values.
Results may differ from the reference program's by a relative error of at most 0.0052.
Values may be sent and summed in bfloat16 or wider, within the bound.
No kernel may reach another device: no remote copies, remote signals or barrier semaphores. Data moves between devices by JAX's collectives and lax.ppermute only.
A program may use at most 128 MiB of HBM per device.

```python
import math
import jax
import jax.numpy as jnp
from jax import lax

E = 1152
BATCH = 20480


def shard_levels(stream_key, dims, cuts, smallest, high):
    def one(axis_at, parts):
        heights = jax.random.uniform(jax.random.fold_in(jax.random.fold_in(stream_key, 6), axis_at), (parts,), jnp.float32, smallest / len(cuts), high / len(cuts))
        return jnp.repeat(jnp.exp(heights), dims[axis_at] // parts).reshape((-1,) + (1,) * (len(dims) - axis_at - 1))

    gain = one(*cuts[0])
    for cut in cuts[1:]:
        gain = gain * one(*cut)
    return gain


def noise(own_key, shape, width, bound, pieces=(), held_as=jnp.bfloat16):
    values = jax.random.normal(own_key, shape, jnp.float32) * width
    if len(pieces) > 0:
        values = shard_levels(own_key, shape, pieces, -0.22, 0.18) * values
    return jnp.clip(values, min=-bound, max=bound).astype(held_as)


def setup_inputs(seed: int = 0) -> dict:
    seeds = jax.random.split(jax.random.key(seed), 6)
    picture_embedding_matrix = noise(seeds[0], (BATCH, E), E ** -0.5, 0.1875, ((0, 128),))
    caption_embedding_matrix = noise(seeds[1], (BATCH, E), E ** -0.5, 0.1875, ((0, 128),))
    matching_caption_indices = jax.random.permutation(seeds[2], BATCH).astype(jnp.int32)
    sharpness_factor = jnp.clip(jnp.exp(jax.random.uniform(seeds[3], (1,), jnp.float32, math.log(5.0), math.log(20.0))), 5.0, 20.0)
    additive_shift_term = jnp.clip(jax.random.uniform(seeds[4], (1,), jnp.float32, -4.0, -1.0), -4.0, -1.0)
    return dict(picture_embedding_matrix=picture_embedding_matrix, caption_embedding_matrix=caption_embedding_matrix, matching_caption_indices=matching_caption_indices, sharpness_factor=sharpness_factor, additive_shift_term=additive_shift_term)


def normalize(raw):
    values = raw.astype(jnp.float32)
    inverse = lax.rsqrt(lax.optimization_barrier(jnp.sum(values * values, axis=1, keepdims=True)) + 1e-06)
    return (values * inverse, inverse)

def backward(unit_grad, unit, inverse):
    along = lax.optimization_barrier(jnp.sum(unit * unit_grad, axis=1, keepdims=True))
    return inverse * (unit_grad - unit * along)

def reference(picture_embedding_matrix, caption_embedding_matrix, matching_caption_indices, sharpness_factor, additive_shift_term):
    image_unit, image_inverse_norm = normalize(picture_embedding_matrix)
    text_unit, text_inverse = normalize(caption_embedding_matrix)
    image_half = image_unit.astype(jnp.bfloat16)
    text_half = text_unit.astype(jnp.bfloat16)
    multiplier_factor = sharpness_factor[0]
    bias_value = additive_shift_term[0]
    text_ids = jnp.arange(BATCH, dtype=jnp.int32)
    rows_per_block = math.gcd(BATCH, 512)
    block_count = BATCH // rows_per_block

    def accumulate(running, block_inputs):
        image_block, block_labels = block_inputs
        logits = multiplier_factor * jnp.dot(image_block, text_half.T, preferred_element_type=jnp.float32) + bias_value
        signs = jnp.where(block_labels[:, None] == text_ids[None, :], 1.0, -1.0).astype(jnp.float32)
        coefficient = (-signs * jax.nn.sigmoid(-signs * logits)).astype(jnp.bfloat16)
        image_part = multiplier_factor * jnp.dot(coefficient, text_half, preferred_element_type=jnp.float32)
        text_part = lax.dot_general(coefficient, image_block, (((0,), (0,)), ((), ())), preferred_element_type=jnp.float32)
        return (running + text_part, image_part)
    opening_total = jnp.zeros((BATCH, E), jnp.float32)
    text_sum, image_parts = lax.scan(accumulate, opening_total, (image_half.reshape(block_count, rows_per_block, E), matching_caption_indices.reshape(block_count, rows_per_block)))
    unit_image_grad = image_parts.reshape(BATCH, E)
    unit_text_grad = multiplier_factor * text_sum
    return (backward(unit_image_grad, image_unit, image_inverse_norm), backward(unit_text_grad, text_unit, text_inverse))
```

```python
import jax
import jax.numpy as jnp
from jax import lax
from jax.experimental import pallas as pl
from jax.experimental.pallas import tpu as pltpu
from jax.sharding import PartitionSpec as P

AXES = ("row", "col")
VMEM = pl.BlockSpec(memory_space=pltpu.VMEM)
SMEM = pl.BlockSpec(memory_space=pltpu.SMEM)
ANY = pl.BlockSpec(memory_space=pl.ANY)
BIG = pltpu.CompilerParams(vmem_limit_bytes=56 * 2**20)
F32 = jnp.float32
BF16 = jnp.bfloat16
BLOCK = 256


def device(x, y, z, k):
    return (y % 4 * 2 + z % 2) * 16 + x % 4 * 4 + z % 4 // 2 * 2 + k


def z_mate(z, k):
    return z + 1 if (z + k) % 2 == 0 else z - 1


def pairs(move):
    out = []
    for x in range(4):
        for y in range(4):
            for z in range(4):
                for k in range(2):
                    out.append((device(x, y, z, k), device(*move(x, y, z, k))))
    return out


def ring(step):
    return pairs(lambda x, y, z, k: (x + step, y, z, k) if k == 0 else (x, y + step, z, k))


CORES = pairs(lambda x, y, z, k: (x, y, z, 1 - k))
MATES = pairs(lambda x, y, z, k: (x, y, z_mate(z, k), k))
STEPS = (0, 1, -1, 2)


def send(value, perm):
    return lax.ppermute(value, AXES, perm)


def normalize(raw):
    values = raw.astype(F32)
    inverse = lax.rsqrt(jnp.sum(values * values, axis=1, keepdims=True) + 1e-06)
    return values * inverse, inverse


def prepare_kernel(place, image, text, labels, keep, away):
    core = place[0]
    rows = image.shape[0]
    image_half = normalize(image[...])[0].astype(BF16)
    text_half = normalize(text[...])[0].astype(BF16)
    label = labels[...]
    high = lax.shift_right_logical(label, 8).astype(F32)
    low = jnp.bitwise_and(label, 255).astype(F32)
    line = lax.broadcasted_iota(jnp.int32, (16, label.shape[1]), 0)
    digits = jnp.where(line == 2 * core, high, jnp.where(line == 2 * core + 1, low, 0.0)).astype(BF16)
    tail = jnp.zeros((16, image.shape[1]), BF16)
    for out in (keep, away):
        out[rows:, :] = tail
        out[rows:, : label.shape[1]] = digits

    @pl.when(core == 0)
    def _():
        keep[:rows, :] = image_half
        away[:rows, :] = text_half

    @pl.when(core == 1)
    def _():
        keep[:rows, :] = text_half
        away[:rows, :] = image_half


def prepare(place, image, text, labels):
    rows, width = image.shape
    shape = jax.ShapeDtypeStruct((rows + 16, width), BF16)
    padded = jnp.pad(labels, (0, 256 - rows)).reshape(1, 256)
    return pl.pallas_call(
        prepare_kernel,
        out_shape=(shape, shape),
        in_specs=[SMEM, VMEM, VMEM, VMEM],
        out_specs=(VMEM, VMEM),
        compiler_params=BIG,
        name="prepare",
    )(place, image, text, padded)


def pair_kernel(pieces, scale, place, *refs):
    mine, other = refs[:pieces], refs[pieces : 2 * pieces]
    keep, away = refs[2 * pieces], refs[2 * pieces + 1]
    images, digits, texts, labels, coefficient, image_out, text_sum, text_out, load_sem, out_sem = refs[
        2 * pieces + 2 :
    ]
    core = place[0]
    rows = mine[0].shape[0] - 16
    half = rows // 2
    block_count = pieces * rows // BLOCK
    text_rows = pieces * half

    def loads(image_from, text_from, offset):
        copies = []
        for p in range(pieces):
            copies.append(
                pltpu.make_async_copy(
                    text_from[p].at[pl.ds(offset, half)], texts.at[pl.ds(p * half, half)], load_sem.at[3 * p]
                )
            )
            copies.append(
                pltpu.make_async_copy(
                    image_from[p].at[pl.ds(0, rows)], images.at[pl.ds(p * rows, rows)], load_sem.at[3 * p + 1]
                )
            )
            copies.append(
                pltpu.make_async_copy(image_from[p].at[pl.ds(rows, 16)], digits.at[p], load_sem.at[3 * p + 2])
            )
        return copies

    @pl.when(core == 0)
    def _():
        for copy in loads(mine, other, half):
            copy.start()
        for copy in loads(mine, other, half):
            copy.wait()

    @pl.when(core == 1)
    def _():
        for copy in loads(other, mine, 0):
            copy.start()
        for copy in loads(other, mine, 0):
            copy.wait()

    text_sum[...] = jnp.zeros_like(text_sum)
    for p in range(pieces):
        digit = digits[p].astype(F32)
        for k in range(2):
            number = digit[2 * k : 2 * k + 1, :half] * 256.0 + digit[2 * k + 1 : 2 * k + 2, :half]
            start = p * rows + k * half
            labels[:, start : start + half] = jnp.broadcast_to(number, (8, half))
    a, b = 0.5 * scale[0], 0.5 * scale[1]
    position = lax.broadcasted_iota(jnp.int32, (half, BLOCK), 0).astype(F32)

    def block(i, _):
        begin = pl.multiple_of(i * BLOCK, BLOCK)
        image = images[pl.ds(begin, BLOCK), :]
        label = labels[0:1, pl.ds(begin, BLOCK)]
        for p in range(pieces):
            logits = lax.dot_general(
                texts[p * half : (p + 1) * half, :], image, (((1,), (1,)), ((), ())), preferred_element_type=F32
            )
            first = place[1 + p].astype(F32)
            shift = jnp.where(position == label - first, -0.5, 0.5)
            coefficient[p * half : (p + 1) * half, :] = (0.5 * jnp.tanh(logits * a + b) + shift).astype(BF16)
        for p in range(text_rows // BLOCK):
            rows_p = slice(p * BLOCK, (p + 1) * BLOCK)
            text_sum[rows_p, :] += jnp.dot(coefficient[rows_p, :], image, preferred_element_type=F32)
        image_out[pl.ds(begin, BLOCK), :] = lax.dot_general(
            coefficient[...], texts[...], (((0,), (0,)), ((), ())), preferred_element_type=F32
        ).astype(BF16)
        return 0

    lax.fori_loop(0, block_count, block, 0)
    text_out[...] = text_sum[...].astype(BF16)

    def flush(image_to, text_to):
        one = pltpu.make_async_copy(image_out, image_to, out_sem.at[0])
        two = pltpu.make_async_copy(text_out, text_to.at[pl.ds(0, text_rows)], out_sem.at[1])
        one.start()
        two.start()
        one.wait()
        two.wait()

    @pl.when(core == 0)
    def _():
        flush(keep, away)

    @pl.when(core == 1)
    def _():
        flush(away, keep)


def pair_sums(scale, place, mine, other):
    pieces = len(mine)
    rows, width = mine[0].shape[0] - 16, mine[0].shape[1]
    total = pieces * rows
    shape = jax.ShapeDtypeStruct((total, width), BF16)
    flops = 6 * total * total // 2 * width
    return pl.pallas_call(
        lambda *refs: pair_kernel(pieces, *refs),
        out_shape=(shape, shape),
        in_specs=[SMEM, SMEM] + [ANY] * (2 * pieces),
        out_specs=(ANY, ANY),
        scratch_shapes=[
            pltpu.VMEM((total, width), BF16),
            pltpu.VMEM((pieces, 16, width), BF16),
            pltpu.VMEM((total // 2, width), BF16),
            pltpu.VMEM((8, total), F32),
            pltpu.VMEM((total // 2, BLOCK), BF16),
            pltpu.VMEM((total, width), BF16),
            pltpu.VMEM((total // 2, width), F32),
            pltpu.VMEM((total // 2, width), BF16),
            pltpu.SemaphoreType.DMA((3 * pieces,)),
            pltpu.SemaphoreType.DMA((2,)),
        ],
        compiler_params=BIG,
        cost_estimate=pl.CostEstimate(flops=flops, bytes_accessed=10 * total * width, transcendentals=total * total // 2),
        name="pair_sums",
    )(scale, place, *mine, *other)


def join_kernel(place, keep, got, *outs):
    core = place[0]
    rows = outs[0].shape[0]
    half = rows // 2

    @pl.when(core == 0)
    def _():
        for p, out in enumerate(outs):
            part = slice(p * rows, (p + 1) * rows)
            out[...] = (keep[part, :].astype(F32) + got[part, :].astype(F32)).astype(BF16)

    @pl.when(core == 1)
    def _():
        for p, out in enumerate(outs):
            part = slice(p * half, (p + 1) * half)
            out[:half, :] = keep[part, :]
            out[half:, :] = got[part, :]


def join(place, keep, got, pieces):
    rows, width = keep.shape[0] // pieces, keep.shape[1]
    shape = jax.ShapeDtypeStruct((rows, width), BF16)
    return pl.pallas_call(
        join_kernel,
        out_shape=(shape,) * pieces,
        in_specs=[SMEM, VMEM, VMEM],
        out_specs=(VMEM,) * pieces,
        compiler_params=BIG,
        name="join",
    )(place, keep, got)


def add_kernel(*refs):
    total = refs[0][...].astype(F32)
    for ref in refs[1:-1]:
        total = total + ref[...].astype(F32)
    refs[-1][...] = total.astype(refs[-1].dtype)


def add(values, dtype):
    return pl.pallas_call(
        add_kernel,
        out_shape=jax.ShapeDtypeStruct(values[0].shape, dtype),
        in_specs=[VMEM] * len(values),
        out_specs=VMEM,
        compiler_params=BIG,
        name="add",
    )(*values)


def finish_kernel(place, scale, image, text, total, got, image_grad, text_grad):
    core = place[0]
    half = got.shape[0]

    def backward(raw, unit_grad):
        unit, inverse = normalize(raw[...])
        unit_grad = scale[0] * unit_grad
        along = jnp.sum(unit * unit_grad, axis=1, keepdims=True)
        return inverse * (unit_grad - unit * along)

    @pl.when(core == 0)
    def _():
        image_grad[...] = backward(image, total[:half, :])
        text_grad[...] = backward(text, got[...])

    @pl.when(core == 1)
    def _():
        image_grad[...] = backward(image, got[...])
        text_grad[...] = backward(text, total[:half, :])


def finish(place, scale, image, text, total, got):
    shape = jax.ShapeDtypeStruct(image.shape, F32)
    return pl.pallas_call(
        finish_kernel,
        out_shape=(shape, shape),
        in_specs=[SMEM, SMEM] + [VMEM] * 4,
        out_specs=(VMEM, VMEM),
        compiler_params=BIG,
        name="finish",
    )(place, scale, image, text, total, got)


def shards(image, text, labels, sharpness, shift):
    rows = image.shape[0]
    row, col = lax.axis_index("row"), lax.axis_index("col")
    x, core = col // 4, col % 2
    y, z = row // 2, col // 2 % 2 * 2 + row % 2
    mate = jnp.where(z % 2 == 1, z + 1, z + 3) % 4
    bases = [device_at(x, y + d, level, core) * rows for level in (z, mate) for d in STEPS]
    place = jnp.stack([core] + bases).astype(jnp.int32)
    scale = jnp.concatenate([sharpness, shift])

    keep, away = prepare(place, image, text, labels)
    got = send(away, CORES)
    own = jnp.concatenate([keep[:rows], got[:rows], keep[rows:] + got[rows:]], axis=0)
    mate_own = send(own, MATES)
    mine = [own] + [send(own, ring(-d)) for d in STEPS[1:]]
    mine += [mate_own] + [send(mate_own, ring(-d)) for d in STEPS[1:]]
    other = [send(piece, CORES) for piece in mine]
    keep, away = pair_sums(scale, place, mine, other)
    got = send(away, CORES)
    parts = join(place, keep, got, 8)
    mate_parts = [parts[4]] + [send(part, ring(d)) for part, d in zip(parts[5:], STEPS[1:])]
    mate_total = send(add(mate_parts, BF16), MATES)
    own_parts = [parts[0]] + [send(part, ring(d)) for part, d in zip(parts[1:4], STEPS[1:])]
    total = add(own_parts + [mate_total], F32)
    got = send(total[rows:], CORES)
    return finish(place, scale, image, text, total, got)


def device_at(x, y, z, k):
    return (y % 4 * 2 + z % 2) * 16 + x % 4 * 4 + z % 4 // 2 * 2 + k


def solution(mesh):
    spec = P(AXES, None)
    return jax.shard_map(
        shards,
        mesh=mesh,
        in_specs=(spec, spec, P(AXES), P(), P()),
        out_specs=(spec, spec),
        check_vma=False,
    )
```

```python
import jax
import jax.numpy as jnp
from jax import lax
from jax.experimental import pallas as pl
from jax.experimental.pallas import tpu as pltpu
from jax.sharding import PartitionSpec as P

AXES = ("row", "col")
VMEM = pl.BlockSpec(memory_space=pltpu.VMEM)
SMEM = pl.BlockSpec(memory_space=pltpu.SMEM)
HBM = pl.BlockSpec(memory_space=pltpu.HBM)
BIG = pltpu.CompilerParams(vmem_limit_bytes=64 * 2**20)
F32 = jnp.float32
BF16 = jnp.bfloat16


def device(x, y, z, k):
    return (y % 4 * 2 + z % 2) * 16 + x % 4 * 4 + z % 4 // 2 * 2 + k


def z_mate(z, k):
    return z + 1 if (z + k) % 2 == 0 else z - 1


def pairs(move):
    out = []
    for x in range(4):
        for y in range(4):
            for z in range(4):
                for k in range(2):
                    out.append((device(x, y, z, k), device(*move(x, y, z, k))))
    return out


def ring(step):
    return pairs(lambda x, y, z, k: (x + step, y, z, k) if k == 0 else (x, y + step, z, k))


CORES = pairs(lambda x, y, z, k: (x, y, z, 1 - k))
MATES = pairs(lambda x, y, z, k: (x, y, z_mate(z, k), k))
STEPS = (0, 1, -1, 2)


def send(value, perm):
    return lax.ppermute(value, AXES, perm)


def normalize(raw):
    values = raw.astype(F32)
    inverse = lax.rsqrt(jnp.sum(values * values, axis=1, keepdims=True) + 1e-06)
    return values * inverse, inverse


def whoami():
    row, col = lax.axis_index("row"), lax.axis_index("col")
    return col // 4, row // 2, col // 2 % 2 * 2 + row % 2, col % 2


def prepare_kernel(image, text, other_image, other_text, labels, other_labels, own):
    core = lax.axis_index("col") % 2
    rows = image.shape[0]

    def fill(mine, other):
        own[:rows, :] = normalize(mine[...])[0].astype(BF16)
        own[rows : 2 * rows, :] = normalize(other[...])[0].astype(BF16)

    @pl.when(core == 0)
    def _():
        fill(image, other_image)

    @pl.when(core == 1)
    def _():
        fill(text, other_text)

    line = lax.broadcasted_iota(jnp.int32, (16, rows), 0)
    digits = jnp.zeros((16, rows), F32)
    for k, label in enumerate((labels[...], other_labels[...])):
        high = lax.shift_right_logical(label, 8).astype(F32)
        low = jnp.bitwise_and(label, 255).astype(F32)
        digits = jnp.where(line == 2 * k, high, jnp.where(line == 2 * k + 1, low, digits))
    own[2 * rows :, :] = jnp.zeros((16, image.shape[1]), BF16)
    own[2 * rows :, :rows] = digits.astype(BF16)


def prepare(image, text, labels):
    rows, width = image.shape
    labels = labels.reshape(1, rows)
    return pl.pallas_call(
        prepare_kernel,
        out_shape=jax.ShapeDtypeStruct((2 * rows + 16, width), BF16),
        in_specs=[VMEM] * 6,
        out_specs=VMEM,
        compiler_params=BIG,
        name="prepare",
    )(image, text, send(image, CORES), send(text, CORES), labels, send(labels, CORES))


class Blocks:
    def __init__(self, mine, other, images, digits, texts, labels, sems):
        self.mine, self.other = mine, other
        self.images, self.digits, self.texts, self.labels, self.sems = images, digits, texts, labels, sems
        self.rows = mine[0].shape[0] - 16
        self.half = self.rows // 2
        self.pieces = len(mine)

    def copies(self, image_from, text_from, offset):
        rows, half = self.rows, self.half
        text, image = [], []
        for p in range(self.pieces):
            text.append((text_from[p].at[pl.ds(offset, half)], self.texts.at[pl.ds(p * half, half)]))
            image.append((image_from[p].at[pl.ds(0, rows)], self.images.at[pl.ds(p * rows, rows)]))
            image.append((image_from[p].at[pl.ds(rows, 16)], self.digits.at[p]))
        return [(a, b, self.sems.at[i]) for i, (a, b) in enumerate(text + image)]

    def each(self, core, wait, which):
        part = {"text": slice(0, self.pieces), "image": slice(self.pieces, None)}[which]

        def act(copies):
            for copy in copies[part]:
                copy = pltpu.make_async_copy(*copy)
                copy.wait() if wait else copy.start()

        @pl.when(core == 0)
        def _():
            act(self.copies(self.mine, self.other, self.half))

        @pl.when(core == 1)
        def _():
            act(self.copies(self.other, self.mine, 0))

    def set_labels(self):
        for p in range(self.pieces):
            digit = self.digits[p].astype(F32)
            for k in range(2):
                number = digit[2 * k : 2 * k + 1, : self.half] * 256.0 + digit[2 * k + 1 : 2 * k + 2, : self.half]
                start = p * self.rows + k * self.half
                self.labels[:, start : start + self.half] = jnp.broadcast_to(number, (8, self.half))


def set_coefficient(scale, mate, texts, images, labels, out):
    a, b = 0.5 * scale[0][0], 0.5 * scale[1][0]
    half = texts.shape[0] // 4
    x, y, z, core = whoami()
    level = jnp.where(mate, jnp.where(z % 2 == 1, z + 1, z + 3) % 4, z)
    logits = lax.dot_general(texts[...], images[...], (((1,), (1,)), ((), ())), preferred_element_type=F32)
    label = labels[0:1, :]
    position = lax.broadcasted_iota(jnp.int32, (half, label.shape[1]), 0).astype(F32)
    for p, step in enumerate(STEPS):
        first = (device_at(x, y + step + 4, level, core) * half).astype(F32)
        part = slice(p * half, (p + 1) * half)
        shift = jnp.where(position == label - first, -0.5, 0.5)
        out[part, :] = (0.5 * jnp.tanh(logits[part, :] * a + b) + shift).astype(BF16)


def device_at(x, y, z, k):
    return (y % 4 * 2 + z % 2) * 16 + x * 4 + z // 2 * 2 + k


def along_text(coefficient, images):
    return jnp.dot(coefficient[...], images[...], preferred_element_type=F32)


def along_image(coefficient, texts):
    return lax.dot_general(coefficient[...], texts[...], (((0,), (0,)), ((), ())), preferred_element_type=F32)


def own_kernel(sharpness, shift, *refs):
    mine, other = refs[:4], refs[4:8]
    image_sum, text_sum = refs[8:10]
    images, digits, labels, texts, coefficient, sems = refs[10:]
    core = lax.axis_index("col") % 2
    group = Blocks(mine, other, images, digits, texts, labels, sems)
    for wait in (False, True):
        group.each(core, wait, "text")
        group.each(core, wait, "image")
    group.set_labels()
    set_coefficient((sharpness, shift), False, texts, images, labels, coefficient)
    text_sum[...] = along_text(coefficient, images)
    image_sum[...] = along_image(coefficient, texts)


def group_scratch(rows, width):
    return [
        pltpu.VMEM((4 * rows, width), BF16),
        pltpu.VMEM((4, 16, width), BF16),
        pltpu.VMEM((8, 4 * rows), F32),
    ]


def cost(quads, rows, width):
    flops = quads * 6 * 8 * rows * rows * width
    return pl.CostEstimate(flops=flops, bytes_accessed=quads * 20 * rows * width, transcendentals=quads * 8 * rows * rows)


def own_sums(scale, mine, other):
    rows, width = mine[0].shape[0] - 16, mine[0].shape[1]
    return pl.pallas_call(
        own_kernel,
        out_shape=(jax.ShapeDtypeStruct((4 * rows, width), F32), jax.ShapeDtypeStruct((2 * rows, width), F32)),
        in_specs=[SMEM] * 2 + [HBM] * 8,
        out_specs=(VMEM, VMEM),
        scratch_shapes=group_scratch(rows, width)
        + [
            pltpu.VMEM((2 * rows, width), BF16),
            pltpu.VMEM((2 * rows, 4 * rows), BF16),
            pltpu.SemaphoreType.DMA((12,)),
        ],
        compiler_params=BIG,
        cost_estimate=cost(1, rows, width),
        name="own_sums",
    )(*scale, *mine, *other)


LEAVING = (((1, 1, 3),), ((0, 1, 2),), ((0, 0, 1), (0, 3, 1), (1, 0, 1)))


def rest_kernel(sharpness, shift, *refs):
    scale = (sharpness, shift)
    own_mine, mate_mine, own_other, mate_other = refs[:4], refs[4:8], refs[8:12], refs[12:16]
    image_before, text_before = refs[16:18]
    keeps, aways = refs[18:21], refs[21:24]
    images, digits, labels, texts, image_total, text_total, coefficient, image_out, text_out = refs[24:33]
    sems, before_sem, out_sem = refs[33:]
    core = lax.axis_index("col") % 2
    rows = own_mine[0].shape[0] - 16
    half = rows // 2
    own = Blocks(own_mine, own_other, images.at[0], digits.at[0], texts.at[0], labels.at[0], sems.at[0])
    mate = Blocks(mate_mine, mate_other, images.at[1], digits.at[1], texts.at[1], labels.at[1], sems.at[1])
    before = [
        pltpu.make_async_copy(image_before, image_total.at[0], before_sem.at[0]),
        pltpu.make_async_copy(text_before, text_total.at[0], before_sem.at[1]),
    ]
    mate.each(core, False, "text")
    own.each(core, False, "image")
    before[0].start()
    own.each(core, False, "text")
    mate.each(core, False, "image")
    before[1].start()
    image_total[1] = jnp.zeros_like(image_total[1])
    text_total[1] = jnp.zeros_like(text_total[1])

    def flush(wait, which):
        def act(image_to, text_to):
            sem = 0
            for g, spans in enumerate(LEAVING):
                at = 0
                for group, first, count in spans:
                    for kind, source, target, size in (
                        (0, image_out, image_to[g], rows),
                        (1, text_out, text_to[g], half),
                    ):
                        if (kind, group) not in which:
                            sem += 1
                            continue
                        copy = pltpu.make_async_copy(
                            source.at[group, pl.ds(first * size, count * size)],
                            target.at[pl.ds(at * size, count * size)],
                            out_sem.at[sem],
                        )
                        copy.wait() if wait else copy.start()
                        sem += 1
                    at += count

        @pl.when(core == 0)
        def _():
            act(keeps, aways)

        @pl.when(core == 1)
        def _():
            act(aways, keeps)

    def block(q, _):
        i = jnp.minimum(q, 1)
        t = 1 - q % 2

        @pl.when(q == 0)
        def _():
            mate.each(core, True, "text")
            own.each(core, True, "image")
            own.set_labels()

        @pl.when(q == 1)
        def _():
            own.each(core, True, "text")
            mate.each(core, True, "image")
            mate.set_labels()
            before[1].wait()
            image_out[0] = image_total[0].astype(BF16)
            flush(False, ((0, 0),))

        @pl.when(q == 2)
        def _():
            text_out[0] = text_total[0].astype(BF16)
            flush(False, ((1, 0),))

        set_coefficient(scale, t == 1, texts.at[t], images.at[i], labels.at[i], coefficient)
        text_total[t] += along_text(coefficient, images.at[i])

        @pl.when(q == 0)
        def _():
            before[0].wait()

        image_total[i] += along_image(coefficient, texts.at[t])
        return 0

    lax.fori_loop(0, 3, block, 0)
    image_out[1] = image_total[1].astype(BF16)
    flush(False, ((0, 1),))
    text_out[1] = text_total[1].astype(BF16)
    flush(False, ((1, 1),))
    flush(True, ((0, 0), (0, 1), (1, 0), (1, 1)))


def rest_sums(scale, mine, other, before):
    rows, width = mine[0].shape[0] - 16, mine[0].shape[1]
    shapes = [jax.ShapeDtypeStruct((sum(n for _, _, n in spans) * rows, width), BF16) for spans in LEAVING]
    outs = pl.pallas_call(
        rest_kernel,
        out_shape=tuple(shapes * 2),
        in_specs=[SMEM] * 2 + [HBM] * 18,
        out_specs=(HBM,) * 6,
        scratch_shapes=[
            pltpu.VMEM((2, 4 * rows, width), BF16),
            pltpu.VMEM((2, 4, 16, width), BF16),
            pltpu.VMEM((2, 8, 4 * rows), F32),
            pltpu.VMEM((2, 2 * rows, width), BF16),
            pltpu.VMEM((2, 4 * rows, width), F32),
            pltpu.VMEM((2, 2 * rows, width), F32),
            pltpu.VMEM((2 * rows, 4 * rows), BF16),
            pltpu.VMEM((2, 4 * rows, width), BF16),
            pltpu.VMEM((2, 2 * rows, width), BF16),
            pltpu.SemaphoreType.DMA((2, 12)),
            pltpu.SemaphoreType.DMA((2,)),
            pltpu.SemaphoreType.DMA((10,)),
        ],
        compiler_params=BIG,
        cost_estimate=cost(3, rows, width),
        name="rest_sums",
    )(*scale, *mine, *other, *before)
    return outs[:3], outs[3:]


def join_kernel(pieces, extras, keep, got, *refs):
    extra, outs = refs[:extras], refs[extras : extras + len(pieces)]
    kept, came, more, sent, sems, out_sems = refs[extras + len(pieces) :]
    core = lax.axis_index("col") % 2
    rows = outs[0].shape[0]
    half = rows // 2

    def loads(size):
        out = []
        for i, p in enumerate(pieces):
            for j, (a, b) in enumerate(((keep, kept), (got, came))):
                out.append(
                    pltpu.make_async_copy(
                        a.at[pl.ds(p * size, size)], b.at[pl.ds(i * rows, size)], sems.at[2 * i + j]
                    )
                )
        return out

    added = [pltpu.make_async_copy(extra[i], more.at[i], out_sems.at[len(pieces) + i]) for i in range(extras)]

    def run(size):
        copies = loads(size)
        for copy in copies + added:
            copy.start()
        stores = []
        for i, out in enumerate(outs):
            copies[2 * i].wait()
            copies[2 * i + 1].wait()
            part = slice(i * rows, (i + 1) * rows)
            first, second = slice(i * rows, i * rows + half), slice(i * rows + half, (i + 1) * rows)
            if i == len(outs) - 1:
                for copy in added:
                    copy.wait()
            if size == rows:
                total = kept[part, :].astype(F32) + came[part, :].astype(F32)
                if extras and i == len(outs) - 1:
                    total = total + more[0].astype(F32)
                sent[part, :] = total.astype(BF16)
            elif extras and i == len(outs) - 1:
                sent[first, :] = (kept[first, :].astype(F32) + more[0, :half, :].astype(F32)).astype(BF16)
                sent[second, :] = (came[first, :].astype(F32) + more[0, half:, :].astype(F32)).astype(BF16)
            else:
                sent[first, :] = kept[first, :]
                sent[second, :] = came[first, :]
            store = pltpu.make_async_copy(sent.at[pl.ds(i * rows, rows)], out, out_sems.at[i])
            store.start()
            stores.append(store)
        for store in stores:
            store.wait()

    @pl.when(core == 0)
    def _():
        run(rows)

    @pl.when(core == 1)
    def _():
        run(half)


def join(keep, got, rows, pieces, extra=()):
    width = keep.shape[1]
    count = len(pieces)
    shape = jax.ShapeDtypeStruct((rows, width), BF16)
    return pl.pallas_call(
        lambda *refs: join_kernel(pieces, len(extra), *refs),
        out_shape=(shape,) * count,
        in_specs=[HBM] * (2 + len(extra)),
        out_specs=(HBM,) * count,
        scratch_shapes=[
            pltpu.VMEM((count * rows, width), BF16),
            pltpu.VMEM((count * rows, width), BF16),
            pltpu.VMEM((1, rows, width), BF16),
            pltpu.VMEM((count * rows, width), BF16),
            pltpu.SemaphoreType.DMA((2 * count,)),
            pltpu.SemaphoreType.DMA((count + 1,)),
        ],
        compiler_params=BIG,
        name="join",
    )(keep, got, *extra)


def total_of(refs):
    total = refs[0][...].astype(F32)
    for ref in refs[1:]:
        total = total + ref[...].astype(F32)
    return total


def add_kernel(*refs):
    refs[-1][...] = total_of(refs[:-1]).astype(refs[-1].dtype)


def add(*values):
    return pl.pallas_call(
        add_kernel,
        out_shape=jax.ShapeDtypeStruct(values[0].shape, BF16),
        in_specs=[VMEM] * len(values),
        out_specs=VMEM,
        compiler_params=BIG,
        name="add",
    )(*values)


def split_kernel(*refs):
    total = total_of(refs[:-2])
    half = total.shape[0] // 2
    refs[-2][...] = total[:half, :]
    refs[-1][...] = total[half:, :]


def split_total(*values):
    shape = jax.ShapeDtypeStruct((values[0].shape[0] // 2, values[0].shape[1]), F32)
    return pl.pallas_call(
        split_kernel,
        out_shape=(shape, shape),
        in_specs=[VMEM] * len(values),
        out_specs=(VMEM, VMEM),
        compiler_params=BIG,
        name="split_total",
    )(*values)


def finish_kernel(scale, image, text, total, got, image_grad, text_grad):
    core = lax.axis_index("col") % 2

    def backward(raw, unit_grad):
        unit, inverse = normalize(raw[...])
        unit_grad = scale[0] * unit_grad[...]
        along = jnp.sum(unit * unit_grad, axis=1, keepdims=True)
        return inverse * (unit_grad - unit * along)

    @pl.when(core == 0)
    def _():
        image_grad[...] = backward(image, total)
        text_grad[...] = backward(text, got)

    @pl.when(core == 1)
    def _():
        image_grad[...] = backward(image, got)
        text_grad[...] = backward(text, total)


def finish(scale, image, text, total, got):
    shape = jax.ShapeDtypeStruct(image.shape, F32)
    return pl.pallas_call(
        finish_kernel,
        out_shape=(shape, shape),
        in_specs=[SMEM] + [VMEM] * 4,
        out_specs=(VMEM, VMEM),
        compiler_params=BIG,
        name="finish",
    )(scale, image, text, total, got)


def after(values, first):
    return lax.optimization_barrier((tuple(values), first))


def after(values, first):
    return list(lax.optimization_barrier((tuple(values), first))[0])


def shards(image, text, labels, sharpness, shift):
    scale = (sharpness, shift)
    rows = 2 * image.shape[0]
    own0 = prepare(image, text, labels)
    mate0 = send(own0, MATES)
    own = [own0] + [send(own0, ring(-d)) for d in STEPS[1:]]
    own = after(own, mate0)
    own_other = [send(piece, CORES) for piece in own]
    mate = [mate0] + [send(mate0, ring(-d)) for d in STEPS[1:3]] + [send(own[3], MATES)]
    before = own_sums(scale, own, own_other)
    mate = after(mate, before)
    mate_other = [send(piece, CORES) for piece in mate]
    keeps, aways = rest_sums(scale, own + mate, own_other + mate_other, before)

    gone = send(aways[0], CORES)
    mate_up, mate_down, far = join(keeps[0], gone, rows, (0, 1, 2))
    far = send(far, MATES)
    mate_up, mate_down = send(mate_up, ring(1)), send(mate_down, ring(-1))
    gone = send(after(aways[1:2], gone)[0], CORES)
    up, down = join(keeps[1], gone, rows, (0, 1))
    up, down = send(up, ring(1)), send(down, ring(-1))
    gone = send(after(aways[2:], gone)[0], CORES)
    own_part, mate_part = join(keeps[2], gone, rows, (0, 2))
    (far,) = join(keeps[2], gone, rows, (1,), (far,))
    far = send(far, ring(2))
    mate_total = send(add(mate_part, mate_up, mate_down), MATES)
    total, away = split_total(own_part, up, down, far, mate_total)
    return finish(sharpness, image, text, total, send(away, CORES))


def solution(mesh):
    spec = P(AXES, None)
    return jax.shard_map(
        shards,
        mesh=mesh,
        in_specs=(spec, spec, P(AXES), P(), P()),
        out_specs=(spec, spec),
        check_vma=False,
    )
```

```python
import jax
import jax.numpy as jnp
from jax import lax
from jax.experimental import pallas as pl
from jax.experimental.pallas import tpu as pltpu
from jax.sharding import PartitionSpec as P

AXES = ("row", "col")
VMEM = pl.BlockSpec(memory_space=pltpu.VMEM)
SMEM = pl.BlockSpec(memory_space=pltpu.SMEM)
HBM = pl.BlockSpec(memory_space=pltpu.HBM)
BIG = pltpu.CompilerParams(vmem_limit_bytes=64 * 2**20)
F32 = jnp.float32
BF16 = jnp.bfloat16


def device(x, y, z, k):
    return (y % 4 * 2 + z % 2) * 16 + x % 4 * 4 + z % 4 // 2 * 2 + k


def z_mate(z, k):
    return z + 1 if (z + k) % 2 == 0 else z - 1


def pairs(move):
    out = []
    for x in range(4):
        for y in range(4):
            for z in range(4):
                for k in range(2):
                    out.append((device(x, y, z, k), device(*move(x, y, z, k))))
    return out


def ring(step):
    return pairs(lambda x, y, z, k: (x + step, y, z, k) if k == 0 else (x, y + step, z, k))


CORES = pairs(lambda x, y, z, k: (x, y, z, 1 - k))
MATES = pairs(lambda x, y, z, k: (x, y, z_mate(z, k), k))
STEPS = (0, 1, -1, 2)
GROUPS = (((0, False), (1, False), (-1, False), (0, True)), ((2, False), (1, True), (-1, True), (2, True)))
CHUNK = 32


def send(value, perm):
    return lax.ppermute(value, AXES, perm)


def normalize(raw):
    values = raw.astype(F32)
    inverse = lax.rsqrt(jnp.sum(values * values, axis=1, keepdims=True) + 1e-06)
    return values * inverse, inverse


def whoami():
    row, col = lax.axis_index("row"), lax.axis_index("col")
    return col // 4, row // 2, col // 2 % 2 * 2 + row % 2, col % 2


def prepare_kernel(image, text, other_image, other_text, labels, other_labels, own):
    core = lax.axis_index("col") % 2
    rows = image.shape[0]

    def fill(mine, other):
        own[:rows, :] = normalize(mine[...])[0].astype(BF16)
        own[rows : 2 * rows, :] = normalize(other[...])[0].astype(BF16)

    @pl.when(core == 0)
    def _():
        fill(image, other_image)

    @pl.when(core == 1)
    def _():
        fill(text, other_text)

    line = lax.broadcasted_iota(jnp.int32, (16, rows), 0)
    digits = jnp.zeros((16, rows), F32)
    for k, label in enumerate((labels[...], other_labels[...])):
        high = lax.shift_right_logical(label, 8).astype(F32)
        low = jnp.bitwise_and(label, 255).astype(F32)
        digits = jnp.where(line == 2 * k, high, jnp.where(line == 2 * k + 1, low, digits))
    own[2 * rows :, :] = jnp.zeros((16, image.shape[1]), BF16)
    own[2 * rows :, :rows] = digits.astype(BF16)


def prepare(image, text, labels):
    rows, width = image.shape
    labels = labels.reshape(1, rows)
    return pl.pallas_call(
        prepare_kernel,
        out_shape=jax.ShapeDtypeStruct((2 * rows + 16, width), BF16),
        in_specs=[VMEM] * 6,
        out_specs=VMEM,
        compiler_params=BIG,
        name="prepare",
    )(image, text, send(image, CORES), send(text, CORES), labels, send(labels, CORES))


class Blocks:
    def __init__(self, mine, other, images, digits, texts, labels, sems):
        self.mine, self.other = mine, other
        self.images, self.digits, self.texts, self.labels, self.sems = images, digits, texts, labels, sems
        self.rows = mine[0].shape[0] - 16
        self.half = self.rows // 2
        self.pieces = len(mine)

    def copies(self, image_from, text_from, offset):
        rows, half = self.rows, self.half
        text, image = [], []
        for p in range(self.pieces):
            text.append((text_from[p].at[pl.ds(offset, half)], self.texts.at[pl.ds(p * half, half)]))
            image.append((image_from[p].at[pl.ds(0, rows)], self.images.at[pl.ds(p * rows, rows)]))
            image.append((image_from[p].at[pl.ds(rows, 16)], self.digits.at[p]))
        return [(a, b, self.sems.at[i]) for i, (a, b) in enumerate(text + image)]

    def each(self, core, wait, which):
        part = {"text": slice(0, self.pieces), "image": slice(self.pieces, None)}[which]

        def act(copies):
            for copy in copies[part]:
                copy = pltpu.make_async_copy(*copy)
                copy.wait() if wait else copy.start()

        @pl.when(core == 0)
        def _():
            act(self.copies(self.mine, self.other, self.half))

        @pl.when(core == 1)
        def _():
            act(self.copies(self.other, self.mine, 0))

    def set_labels(self):
        for p in range(self.pieces):
            digit = self.digits[p].astype(F32)
            for k in range(2):
                number = digit[2 * k : 2 * k + 1, : self.half] * 256.0 + digit[2 * k + 1 : 2 * k + 2, : self.half]
                start = p * self.rows + k * self.half
                self.labels[:, start : start + self.half] = jnp.broadcast_to(number, (8, self.half))


def set_coefficient(scale, late, texts, images, labels, out):
    a, b = 0.5 * scale[0][0], 0.5 * scale[1][0]
    half = texts.shape[0] // 4
    x, y, z, core = whoami()
    mate_z = jnp.where(z % 2 == 1, z + 1, z + 3) % 4
    logits = lax.dot_general(texts[...], images[...], (((1,), (1,)), ((), ())), preferred_element_type=F32)
    label = labels[0:1, :]
    position = lax.broadcasted_iota(jnp.int32, (half, label.shape[1]), 0).astype(F32)
    for p in range(4):
        (near_step, near_mate), (far_step, far_mate) = GROUPS[0][p], GROUPS[1][p]
        one = device_at(x, y + near_step + 4, mate_z if near_mate else z, core)
        two = device_at(x, y + far_step + 4, mate_z if far_mate else z, core)
        first = (jnp.where(late, two, one) * half).astype(F32)
        part = slice(p * half, (p + 1) * half)
        shift = jnp.where(position == label - first, -0.5, 0.5)
        out[part, :] = (0.5 * jnp.tanh(logits[part, :] * a + b) + shift).astype(BF16)


def device_at(x, y, z, k):
    return (y % 4 * 2 + z % 2) * 16 + x * 4 + z // 2 * 2 + k


def along_text(coefficient, images):
    return jnp.dot(coefficient[...], images[...], preferred_element_type=F32)


def along_image(coefficient, texts):
    return lax.dot_general(coefficient[...], texts[...], (((0,), (0,)), ((), ())), preferred_element_type=F32)


def own_kernel(sharpness, shift, *refs):
    mine, other = refs[:4], refs[4:8]
    image_to, text_to = refs[8:10]
    images, digits, labels, texts, coefficient, image_sum, text_sum, sems, out_sem = refs[10:]
    core = lax.axis_index("col") % 2
    group = Blocks(mine, other, images, digits, texts, labels, sems)
    for wait in (False, True):
        group.each(core, wait, "text")
        group.each(core, wait, "image")
    group.set_labels()
    set_coefficient((sharpness, shift), False, texts, images, labels, coefficient)
    text_sum[...] = along_text(coefficient, images)
    copies = [pltpu.make_async_copy(text_sum, text_to, out_sem.at[0])]
    copies[0].start()
    part = images.shape[0] // 2
    for i in range(2):
        here = pl.ds(i * part, part)
        image_sum[here, :] = along_image(coefficient.at[:, here], texts)
        copies.append(pltpu.make_async_copy(image_sum.at[here], image_to.at[here], out_sem.at[1 + i]))
        copies[-1].start()
    for copy in copies:
        copy.wait()


def group_scratch(rows, width):
    return [
        pltpu.VMEM((4 * rows, width), BF16),
        pltpu.VMEM((4, 16, width), BF16),
        pltpu.VMEM((8, 4 * rows), F32),
    ]


def cost(quads, rows, width):
    flops = quads * 6 * 8 * rows * rows * width
    return pl.CostEstimate(flops=flops, bytes_accessed=quads * 20 * rows * width, transcendentals=quads * 8 * rows * rows)


def own_sums(scale, mine, other):
    rows, width = mine[0].shape[0] - 16, mine[0].shape[1]
    return pl.pallas_call(
        own_kernel,
        out_shape=(jax.ShapeDtypeStruct((4 * rows, width), F32), jax.ShapeDtypeStruct((2 * rows, width), F32)),
        in_specs=[SMEM] * 2 + [HBM] * 8,
        out_specs=(HBM, HBM),
        scratch_shapes=group_scratch(rows, width)
        + [
            pltpu.VMEM((2 * rows, width), BF16),
            pltpu.VMEM((2 * rows, 4 * rows), BF16),
            pltpu.VMEM((4 * rows, width), F32),
            pltpu.VMEM((2 * rows, width), F32),
            pltpu.SemaphoreType.DMA((12,)),
            pltpu.SemaphoreType.DMA((3,)),
        ],
        compiler_params=BIG,
        cost_estimate=cost(1, rows, width),
        name="own_sums",
    )(*scale, *mine, *other)


LEAVING = (((1, 1, 3),), ((0, 1, 2),), ((0, 0, 1), (1, 0, 1), (0, 3, 1)))


def rest_kernel(sharpness, shift, *refs):
    scale = (sharpness, shift)
    own_mine, mate_mine, own_other, mate_other = refs[:4], refs[4:8], refs[8:12], refs[12:16]
    image_before, text_before = refs[16:18]
    keeps, aways = refs[18:21], refs[21:24]
    images, digits, labels, texts, image_total, text_total, coefficient, image_out, text_out = refs[24:33]
    sems, before_sem, out_sem = refs[33:]
    core = lax.axis_index("col") % 2
    rows = own_mine[0].shape[0] - 16
    half = rows // 2
    own = Blocks(own_mine, own_other, images.at[0], digits.at[0], texts.at[0], labels.at[0], sems.at[0])
    mate = Blocks(mate_mine, mate_other, images.at[1], digits.at[1], texts.at[1], labels.at[1], sems.at[1])
    before = [
        pltpu.make_async_copy(image_before, image_total.at[0], before_sem.at[0]),
        pltpu.make_async_copy(text_before, text_total.at[0], before_sem.at[1]),
    ]
    mate.each(core, False, "text")
    own.each(core, False, "image")
    before[0].start()
    own.each(core, False, "text")
    mate.each(core, False, "image")
    before[1].start()
    image_total[1] = jnp.zeros_like(image_total[1])
    text_total[1] = jnp.zeros_like(text_total[1])

    def flush(wait, which):
        def act(image_to, text_to):
            sem = 0
            for g, spans in enumerate(LEAVING):
                at = 0
                for group, first, count in spans:
                    for kind, source, target, size in (
                        (0, image_out, image_to[g], rows),
                        (1, text_out, text_to[g], half),
                    ):
                        if (kind, group) not in which:
                            sem += 1
                            continue
                        copy = pltpu.make_async_copy(
                            source.at[group, pl.ds(first * size, count * size)],
                            target.at[pl.ds(at * size, count * size)],
                            out_sem.at[sem],
                        )
                        copy.wait() if wait else copy.start()
                        sem += 1
                    at += count

        @pl.when(core == 0)
        def _():
            act(keeps, aways)

        @pl.when(core == 1)
        def _():
            act(aways, keeps)

    def block(q, _):
        i = jnp.minimum(q, 1)
        t = 1 - q % 2

        @pl.when(q == 0)
        def _():
            mate.each(core, True, "text")
            own.each(core, True, "image")
            own.set_labels()

        @pl.when(q == 1)
        def _():
            own.each(core, True, "text")
            mate.each(core, True, "image")
            mate.set_labels()
            before[1].wait()
            image_out[0] = image_total[0].astype(BF16)
            flush(False, ((0, 0),))

        @pl.when(q == 2)
        def _():
            text_out[0] = text_total[0].astype(BF16)
            flush(False, ((1, 0),))

        set_coefficient(scale, t == 1, texts.at[t], images.at[i], labels.at[i], coefficient)
        text_total[t] += along_text(coefficient, images.at[i])

        @pl.when(q == 0)
        def _():
            before[0].wait()

        @pl.when(q == 2)
        def _():
            text_out[1] = text_total[1].astype(BF16)
            flush(False, ((1, 1),))

        image_total[i] += along_image(coefficient, texts.at[t])
        return 0

    lax.fori_loop(0, 3, block, 0)
    image_out[1] = image_total[1].astype(BF16)
    flush(False, ((0, 1),))
    flush(True, ((0, 0), (0, 1), (1, 0), (1, 1)))


def rest_sums(scale, mine, other, before):
    rows, width = mine[0].shape[0] - 16, mine[0].shape[1]
    shapes = [jax.ShapeDtypeStruct((sum(n for _, _, n in spans) * rows, width), BF16) for spans in LEAVING]
    outs = pl.pallas_call(
        rest_kernel,
        out_shape=tuple(shapes * 2),
        in_specs=[SMEM] * 2 + [HBM] * 18,
        out_specs=(HBM,) * 6,
        scratch_shapes=[
            pltpu.VMEM((2, 4 * rows, width), BF16),
            pltpu.VMEM((2, 4, 16, width), BF16),
            pltpu.VMEM((2, 8, 4 * rows), F32),
            pltpu.VMEM((2, 2 * rows, width), BF16),
            pltpu.VMEM((2, 4 * rows, width), F32),
            pltpu.VMEM((2, 2 * rows, width), F32),
            pltpu.VMEM((2 * rows, 4 * rows), BF16),
            pltpu.VMEM((2, 4 * rows, width), BF16),
            pltpu.VMEM((2, 2 * rows, width), BF16),
            pltpu.SemaphoreType.DMA((2, 12)),
            pltpu.SemaphoreType.DMA((2,)),
            pltpu.SemaphoreType.DMA((10,)),
        ],
        compiler_params=BIG,
        cost_estimate=cost(3, rows, width),
        name="rest_sums",
    )(*scale, *mine, *other, *before)
    return outs[:3], outs[3:]


def join_kernel(pieces, extras, keep, got, *refs):
    extra, outs = refs[:extras], refs[extras : extras + len(pieces)]
    kept, came, more, sent, sems, out_sems = refs[extras + len(pieces) :]
    core = lax.axis_index("col") % 2
    rows = outs[0].shape[0]
    half = rows // 2

    def loads(size):
        out = []
        for i, p in enumerate(pieces):
            for j, (a, b) in enumerate(((keep, kept), (got, came))):
                out.append(
                    pltpu.make_async_copy(
                        a.at[pl.ds(p * size, size)], b.at[pl.ds(i * rows, size)], sems.at[2 * i + j]
                    )
                )
        return out

    added = [pltpu.make_async_copy(extra[i], more.at[i], out_sems.at[len(pieces) + i]) for i in range(extras)]

    def run(size):
        copies = loads(size)
        for copy in copies + added:
            copy.start()
        stores = []
        for i, out in enumerate(outs):
            copies[2 * i].wait()
            copies[2 * i + 1].wait()
            last = extras and i == len(outs) - 1
            if last:
                for copy in added:
                    copy.wait()

            def chunk(c, _):
                here = pl.ds(pl.multiple_of(i * rows + c * CHUNK, CHUNK), CHUNK)
                there = pl.ds(pl.multiple_of(i * rows + half + c * CHUNK, CHUNK), CHUNK)
                if size == rows:
                    total = kept[here, :].astype(F32) + came[here, :].astype(F32)
                    if last:
                        total = total + more[0, pl.ds(pl.multiple_of(c * CHUNK, CHUNK), CHUNK), :].astype(F32)
                    sent[here, :] = total.astype(BF16)
                    return 0
                for source, target, offset in ((kept, here, 0), (came, there, half)):
                    value = source[here, :]
                    if last:
                        extra_rows = pl.ds(pl.multiple_of(offset + c * CHUNK, CHUNK), CHUNK)
                        value = (value.astype(F32) + more[0, extra_rows, :].astype(F32)).astype(BF16)
                    sent[target, :] = value
                return 0

            lax.fori_loop(0, size // CHUNK, chunk, 0)
            store = pltpu.make_async_copy(sent.at[pl.ds(i * rows, rows)], out, out_sems.at[i])
            store.start()
            stores.append(store)
        for store in stores:
            store.wait()

    @pl.when(core == 0)
    def _():
        run(rows)

    @pl.when(core == 1)
    def _():
        run(half)


def join(keep, got, rows, pieces, extra=()):
    width = keep.shape[1]
    count = len(pieces)
    shape = jax.ShapeDtypeStruct((rows, width), BF16)
    return pl.pallas_call(
        lambda *refs: join_kernel(pieces, len(extra), *refs),
        out_shape=(shape,) * count,
        in_specs=[HBM] * (2 + len(extra)),
        out_specs=(HBM,) * count,
        scratch_shapes=[
            pltpu.VMEM((count * rows, width), BF16),
            pltpu.VMEM((count * rows, width), BF16),
            pltpu.VMEM((1, rows, width), BF16),
            pltpu.VMEM((count * rows, width), BF16),
            pltpu.SemaphoreType.DMA((2 * count,)),
            pltpu.SemaphoreType.DMA((count + 1,)),
        ],
        compiler_params=BIG,
        name="join",
    )(keep, got, *extra)


def each_chunk(rows, step):
    def run(c, _):
        step(pl.ds(pl.multiple_of(c * CHUNK, CHUNK), CHUNK), c)
        return 0

    lax.fori_loop(0, rows // CHUNK, run, 0)


def total_of(refs, part):
    total = refs[0][part, :].astype(F32)
    for ref in refs[1:]:
        total = total + ref[part, :].astype(F32)
    return total


def add_kernel(*refs):
    def step(part, c):
        refs[-1][part, :] = total_of(refs[:-1], part).astype(refs[-1].dtype)

    each_chunk(refs[-1].shape[0], step)


def add(*values):
    return pl.pallas_call(
        add_kernel,
        out_shape=jax.ShapeDtypeStruct(values[0].shape, BF16),
        in_specs=[VMEM] * len(values),
        out_specs=VMEM,
        compiler_params=BIG,
        name="add",
    )(*values)


def split_kernel(*refs):
    half = refs[-1].shape[0]

    def step(part, c):
        refs[-2][part, :] = total_of(refs[:-2], part)
        other = pl.ds(pl.multiple_of(half + c * CHUNK, CHUNK), CHUNK)
        refs[-1][part, :] = total_of(refs[:-2], other)

    each_chunk(half, step)


def split_total(*values):
    shape = jax.ShapeDtypeStruct((values[0].shape[0] // 2, values[0].shape[1]), F32)
    return pl.pallas_call(
        split_kernel,
        out_shape=(shape, shape),
        in_specs=[VMEM] * len(values),
        out_specs=(VMEM, VMEM),
        compiler_params=BIG,
        name="split_total",
    )(*values)


def finish_kernel(scale, image, text, kept, got, far, last, got_far, got_last, image_grad, text_grad):
    core = lax.axis_index("col") % 2

    def backward(raw, parts):
        unit, inverse = normalize(raw[...])
        unit_grad = scale[0] * (parts[0][...] + parts[1][...].astype(F32) + parts[2][...].astype(F32))
        along = jnp.sum(unit * unit_grad, axis=1, keepdims=True)
        return inverse * (unit_grad - unit * along)

    @pl.when(core == 0)
    def _():
        image_grad[...] = backward(image, (kept, far, last))
        text_grad[...] = backward(text, (got, got_far, got_last))

    @pl.when(core == 1)
    def _():
        image_grad[...] = backward(image, (got, got_far, got_last))
        text_grad[...] = backward(text, (kept, far, last))


def finish(scale, image, text, kept, got, far, last):
    rows, width = image.shape
    shape = jax.ShapeDtypeStruct(image.shape, F32)
    block = pl.BlockSpec((rows // 2, width), lambda i: (i, 0))
    other = pl.BlockSpec((rows // 2, width), lambda i: (2 + i, 0))
    return pl.pallas_call(
        finish_kernel,
        grid=(2,),
        out_shape=(shape, shape),
        in_specs=[SMEM] + [block] * 6 + [other] * 2,
        out_specs=(block, block),
        compiler_params=BIG,
        name="finish",
    )(scale, image, text, kept, got, far, last, send(far, CORES), send(last, CORES))


def after(values, first):
    return lax.optimization_barrier((tuple(values), first))


def after(values, first):
    return list(lax.optimization_barrier((tuple(values), first))[0])


def shards(image, text, labels, sharpness, shift):
    scale = (sharpness, shift)
    rows = 2 * image.shape[0]
    own0 = prepare(image, text, labels)
    mate0 = send(own0, MATES)
    up, down, far = (send(own0, ring(-d)) for d in STEPS[1:])
    own = [own0, up, down, mate0]
    own_other = [send(piece, CORES) for piece in own]
    mate = [far] + [send(mate0, ring(-d)) for d in STEPS[1:3]] + [send(far, MATES)]
    before = own_sums(scale, own, own_other)
    mate = mate[:1] + after(mate[1:], before)
    mate_other = [send(piece, CORES) for piece in mate]
    keeps, aways = rest_sums(scale, own + mate, own_other + mate_other, before)

    gone = send(aways[0], CORES)
    own_gone, last_gone = (send(away, CORES) for away in after(aways[1:], gone))
    mate_up, mate_down, far = join(keeps[0], gone, rows, (0, 1, 2))
    far = send(far, MATES)
    mate_up, mate_down = send(mate_up, ring(1)), send(mate_down, ring(-1))
    up, down = join(keeps[1], own_gone, rows, (0, 1))
    up, down = send(up, ring(1)), send(down, ring(-1))
    (far,) = join(keeps[2], last_gone, rows, (1,), (far,))
    own_part, mate_part = join(keeps[2], last_gone, rows, (0, 2))
    (mate_part,) = after((mate_part,), far)
    far = send(far, ring(2))
    mate_total = send(add(mate_part, mate_up, mate_down), MATES)
    kept, away = split_total(own_part, up, down)
    return finish(sharpness, image, text, kept, send(away, CORES), far, mate_total)


def solution(mesh):
    spec = P(AXES, None)
    return jax.shard_map(
        shards,
        mesh=mesh,
        in_specs=(spec, spec, P(AXES), P(), P()),
        out_specs=(spec, spec),
        check_vma=False,
    )
```

```python
import jax
import jax.numpy as jnp
from jax import lax
from jax.experimental import pallas as pl
from jax.experimental.pallas import tpu as pltpu
from jax.sharding import PartitionSpec as P

AXES = ("row", "col")
VMEM = pl.BlockSpec(memory_space=pltpu.VMEM)
SMEM = pl.BlockSpec(memory_space=pltpu.SMEM)
HBM = pl.BlockSpec(memory_space=pltpu.HBM)
BIG = pltpu.CompilerParams(vmem_limit_bytes=64 * 2**20)
F32 = jnp.float32
BF16 = jnp.bfloat16


def device(x, y, z, k):
    return (y % 4 * 2 + z % 2) * 16 + x % 4 * 4 + z % 4 // 2 * 2 + k


def z_mate(z, k):
    return z + 1 if (z + k) % 2 == 0 else z - 1


def pairs(move):
    out = []
    for x in range(4):
        for y in range(4):
            for z in range(4):
                for k in range(2):
                    out.append((device(x, y, z, k), device(*move(x, y, z, k))))
    return out


def ring(step):
    return pairs(lambda x, y, z, k: (x + step, y, z, k) if k == 0 else (x, y + step, z, k))


CORES = pairs(lambda x, y, z, k: (x, y, z, 1 - k))
MATES = pairs(lambda x, y, z, k: (x, y, z_mate(z, k), k))
STEPS = (0, 1, -1, 2)
GROUPS = (((0, False), (1, False), (-1, False), (0, True)), ((2, False), (1, True), (-1, True), (2, True)))
CHUNK = 32


def send(value, perm):
    return lax.ppermute(value, AXES, perm)


def normalize(raw):
    values = raw.astype(F32)
    inverse = lax.rsqrt(jnp.sum(values * values, axis=1, keepdims=True) + 1e-06)
    return values * inverse, inverse


def whoami():
    row, col = lax.axis_index("row"), lax.axis_index("col")
    return col // 4, row // 2, col // 2 % 2 * 2 + row % 2, col % 2


def prepare_kernel(image, text, other_image, other_text, labels, other_labels, own):
    core = lax.axis_index("col") % 2
    rows = image.shape[0]

    def fill(mine, other):
        own[:rows, :] = normalize(mine[...])[0].astype(BF16)
        own[rows : 2 * rows, :] = normalize(other[...])[0].astype(BF16)

    @pl.when(core == 0)
    def _():
        fill(image, other_image)

    @pl.when(core == 1)
    def _():
        fill(text, other_text)

    line = lax.broadcasted_iota(jnp.int32, (16, rows), 0)
    digits = jnp.zeros((16, rows), F32)
    for k, label in enumerate((labels[...], other_labels[...])):
        high = lax.shift_right_logical(label, 8).astype(F32)
        low = jnp.bitwise_and(label, 255).astype(F32)
        digits = jnp.where(line == 2 * k, high, jnp.where(line == 2 * k + 1, low, digits))
    own[2 * rows :, :] = jnp.zeros((16, image.shape[1]), BF16)
    own[2 * rows :, :rows] = digits.astype(BF16)


def prepare(image, text, labels):
    rows, width = image.shape
    labels = labels.reshape(1, rows)
    return pl.pallas_call(
        prepare_kernel,
        out_shape=jax.ShapeDtypeStruct((2 * rows + 16, width), BF16),
        in_specs=[VMEM] * 6,
        out_specs=VMEM,
        compiler_params=BIG,
        name="prepare",
    )(image, text, send(image, CORES), send(text, CORES), labels, send(labels, CORES))


class Blocks:
    def __init__(self, mine, other, images, digits, texts, labels, sems):
        self.mine, self.other = mine, other
        self.images, self.digits, self.texts, self.labels, self.sems = images, digits, texts, labels, sems
        self.rows = mine[0].shape[0] - 16
        self.half = self.rows // 2
        self.pieces = len(mine)

    def copies(self, image_from, text_from, offset):
        rows, half = self.rows, self.half
        text, image = [], []
        for p in range(self.pieces):
            text.append((text_from[p].at[pl.ds(offset, half)], self.texts.at[pl.ds(p * half, half)]))
            image.append((image_from[p].at[pl.ds(0, rows)], self.images.at[pl.ds(p * rows, rows)]))
            image.append((image_from[p].at[pl.ds(rows, 16)], self.digits.at[p]))
        return [(a, b, self.sems.at[i]) for i, (a, b) in enumerate(text + image)]

    def each(self, core, wait, which):
        part = {"text": slice(0, self.pieces), "image": slice(self.pieces, None)}[which]

        def act(copies):
            for copy in copies[part]:
                copy = pltpu.make_async_copy(*copy)
                copy.wait() if wait else copy.start()

        @pl.when(core == 0)
        def _():
            act(self.copies(self.mine, self.other, self.half))

        @pl.when(core == 1)
        def _():
            act(self.copies(self.other, self.mine, 0))

    def set_labels(self):
        for p in range(self.pieces):
            digit = self.digits[p].astype(F32)
            for k in range(2):
                number = digit[2 * k : 2 * k + 1, : self.half] * 256.0 + digit[2 * k + 1 : 2 * k + 2, : self.half]
                start = p * self.rows + k * self.half
                self.labels[:, start : start + self.half] = jnp.broadcast_to(number, (8, self.half))


def set_coefficient(scale, late, texts, images, labels, out):
    a, b = 0.5 * scale[0][0], 0.5 * scale[1][0]
    half = texts.shape[0] // 4
    x, y, z, core = whoami()
    mate_z = jnp.where(z % 2 == 1, z + 1, z + 3) % 4
    logits = lax.dot_general(texts[...], images[...], (((1,), (1,)), ((), ())), preferred_element_type=F32)
    label = labels[0:1, :]
    position = lax.broadcasted_iota(jnp.int32, (half, label.shape[1]), 0).astype(F32)
    for p in range(4):
        (near_step, near_mate), (far_step, far_mate) = GROUPS[0][p], GROUPS[1][p]
        one = device_at(x, y + near_step + 4, mate_z if near_mate else z, core)
        two = device_at(x, y + far_step + 4, mate_z if far_mate else z, core)
        first = (jnp.where(late, two, one) * half).astype(F32)
        part = slice(p * half, (p + 1) * half)
        shift = jnp.where(position == label - first, -0.5, 0.5)
        out[part, :] = (0.5 * jnp.tanh(logits[part, :] * a + b) + shift).astype(BF16)


def device_at(x, y, z, k):
    return (y % 4 * 2 + z % 2) * 16 + x * 4 + z // 2 * 2 + k


def along_text(coefficient, images):
    return jnp.dot(coefficient[...], images[...], preferred_element_type=F32)


def along_image(coefficient, texts):
    return lax.dot_general(coefficient[...], texts[...], (((0,), (0,)), ((), ())), preferred_element_type=F32)


def own_kernel(sharpness, shift, *refs):
    mine, other = refs[:4], refs[4:8]
    image_to, text_to = refs[8:10]
    images, digits, labels, texts, coefficient, image_sum, text_sum, sems, out_sem = refs[10:]
    core = lax.axis_index("col") % 2
    group = Blocks(mine, other, images, digits, texts, labels, sems)
    for wait in (False, True):
        group.each(core, wait, "text")
        group.each(core, wait, "image")
    group.set_labels()
    set_coefficient((sharpness, shift), False, texts, images, labels, coefficient)
    text_sum[...] = along_text(coefficient, images)
    copies = [pltpu.make_async_copy(text_sum, text_to, out_sem.at[0])]
    copies[0].start()
    part = images.shape[0] // 2
    for i in range(2):
        here = pl.ds(i * part, part)
        image_sum[here, :] = along_image(coefficient.at[:, here], texts)
        copies.append(pltpu.make_async_copy(image_sum.at[here], image_to.at[here], out_sem.at[1 + i]))
        copies[-1].start()
    for copy in copies:
        copy.wait()


def group_scratch(rows, width):
    return [
        pltpu.VMEM((4 * rows, width), BF16),
        pltpu.VMEM((4, 16, width), BF16),
        pltpu.VMEM((8, 4 * rows), F32),
    ]


def cost(quads, rows, width):
    flops = quads * 6 * 8 * rows * rows * width
    return pl.CostEstimate(flops=flops, bytes_accessed=quads * 20 * rows * width, transcendentals=quads * 8 * rows * rows)


def own_sums(scale, mine, other):
    rows, width = mine[0].shape[0] - 16, mine[0].shape[1]
    return pl.pallas_call(
        own_kernel,
        out_shape=(jax.ShapeDtypeStruct((4 * rows, width), F32), jax.ShapeDtypeStruct((2 * rows, width), F32)),
        in_specs=[SMEM] * 2 + [HBM] * 8,
        out_specs=(HBM, HBM),
        scratch_shapes=group_scratch(rows, width)
        + [
            pltpu.VMEM((2 * rows, width), BF16),
            pltpu.VMEM((2 * rows, 4 * rows), BF16),
            pltpu.VMEM((4 * rows, width), F32),
            pltpu.VMEM((2 * rows, width), F32),
            pltpu.SemaphoreType.DMA((12,)),
            pltpu.SemaphoreType.DMA((3,)),
        ],
        compiler_params=BIG,
        cost_estimate=cost(1, rows, width),
        name="own_sums",
    )(*scale, *mine, *other)


LEAVING = (((1, 1, 1), (1, 2, 2)), ((0, 1, 2),), ((0, 0, 1), (1, 0, 1), (0, 3, 1)))


def rest_kernel(sharpness, shift, *refs):
    scale = (sharpness, shift)
    own_mine, mate_mine, own_other, mate_other = refs[:4], refs[4:8], refs[8:12], refs[12:16]
    image_before, text_before = refs[16:18]
    keeps, aways = refs[18:21], refs[21:24]
    images, digits, labels, texts, image_total, text_total, coefficient, image_out, text_out = refs[24:33]
    sems, before_sem, out_sem = refs[33:]
    core = lax.axis_index("col") % 2
    rows = own_mine[0].shape[0] - 16
    half = rows // 2
    own = Blocks(own_mine, own_other, images.at[0], digits.at[0], texts.at[0], labels.at[0], sems.at[0])
    mate = Blocks(mate_mine, mate_other, images.at[1], digits.at[1], texts.at[1], labels.at[1], sems.at[1])
    before = [
        pltpu.make_async_copy(image_before, image_total.at[0], before_sem.at[0]),
        pltpu.make_async_copy(text_before, text_total.at[0], before_sem.at[1]),
    ]
    mate.each(core, False, "text")
    own.each(core, False, "image")
    image_total[1] = jnp.zeros_like(image_total[1])
    text_total[1] = jnp.zeros_like(text_total[1])

    def flush(wait, wanted):
        def act(image_to, text_to):
            sem = 0
            for g, spans in enumerate(LEAVING):
                at = 0
                for group, first, count in spans:
                    for kind, source, target, size in (
                        (0, image_out, image_to[g], rows),
                        (1, text_out, text_to[g], half),
                    ):
                        if not wanted(kind, group, first):
                            sem += 1
                            continue
                        copy = pltpu.make_async_copy(
                            source.at[group, pl.ds(first * size, count * size)],
                            target.at[pl.ds(at * size, count * size)],
                            out_sem.at[sem],
                        )
                        copy.wait() if wait else copy.start()
                        sem += 1
                    at += count

        @pl.when(core == 0)
        def _():
            act(keeps, aways)

        @pl.when(core == 1)
        def _():
            act(aways, keeps)

    def block(q, _):
        i = jnp.minimum(q, 1)
        t = 1 - q % 2

        @pl.when(q == 0)
        def _():
            mate.each(core, True, "text")
            own.each(core, True, "image")
            before[0].start()
            own.each(core, False, "text")
            mate.each(core, False, "image")
            before[1].start()
            own.set_labels()

        @pl.when(q == 1)
        def _():
            own.each(core, True, "text")
            mate.each(core, True, "image")
            mate.set_labels()
            before[1].wait()

        set_coefficient(scale, t == 1, texts.at[t], images.at[i], labels.at[i], coefficient)
        text_sum = text_total[t] + along_text(coefficient, images.at[i])
        text_total[t] = text_sum
        text_out[t] = text_sum.astype(BF16)

        @pl.when(q == 0)
        def _():
            before[0].wait()

        @pl.when(q == 1)
        def _():
            flush(False, lambda kind, group, first: kind == 1 and group == 0)

        @pl.when(q == 2)
        def _():
            flush(False, lambda kind, group, first: kind == 1 and group == 1)

        for h in range(2):
            here = pl.ds(2 * h * rows, 2 * rows)
            image_sum = image_total[i, here, :] + along_image(coefficient.at[:, here], texts.at[t])
            image_total[i, here, :] = image_sum
            image_out[i, here, :] = image_sum.astype(BF16)

            if h == 0:

                @pl.when(q == 2)
                def _():
                    flush(False, lambda kind, group, first: kind == 0 and group == 1 and first < 2)

        @pl.when(q == 0)
        def _():
            flush(False, lambda kind, group, first: kind == 0 and group == 0)

        return 0

    lax.fori_loop(0, 3, block, 0)
    flush(False, lambda kind, group, first: kind == 0 and group == 1 and first >= 2)
    flush(True, lambda kind, group, first: True)


def rest_sums(scale, mine, other, before):
    rows, width = mine[0].shape[0] - 16, mine[0].shape[1]
    shapes = [jax.ShapeDtypeStruct((sum(n for _, _, n in spans) * rows, width), BF16) for spans in LEAVING]
    outs = pl.pallas_call(
        rest_kernel,
        out_shape=tuple(shapes * 2),
        in_specs=[SMEM] * 2 + [HBM] * 18,
        out_specs=(HBM,) * 6,
        scratch_shapes=[
            pltpu.VMEM((2, 4 * rows, width), BF16),
            pltpu.VMEM((2, 4, 16, width), BF16),
            pltpu.VMEM((2, 8, 4 * rows), F32),
            pltpu.VMEM((2, 2 * rows, width), BF16),
            pltpu.VMEM((2, 4 * rows, width), F32),
            pltpu.VMEM((2, 2 * rows, width), F32),
            pltpu.VMEM((2 * rows, 4 * rows), BF16),
            pltpu.VMEM((2, 4 * rows, width), BF16),
            pltpu.VMEM((2, 2 * rows, width), BF16),
            pltpu.SemaphoreType.DMA((2, 12)),
            pltpu.SemaphoreType.DMA((2,)),
            pltpu.SemaphoreType.DMA((12,)),
        ],
        compiler_params=BIG,
        cost_estimate=cost(3, rows, width),
        name="rest_sums",
    )(*scale, *mine, *other, *before)
    return outs[:3], outs[3:]


def join_kernel(pieces, extras, keep, got, *refs):
    extra, outs = refs[:extras], refs[extras : extras + len(pieces)]
    kept, came, more, sent, sems, out_sems = refs[extras + len(pieces) :]
    core = lax.axis_index("col") % 2
    rows = outs[0].shape[0]
    half = rows // 2

    def loads(size):
        out = []
        for i, p in enumerate(pieces):
            for j, (a, b) in enumerate(((keep, kept), (got, came))):
                out.append(
                    pltpu.make_async_copy(
                        a.at[pl.ds(p * size, size)], b.at[pl.ds(i * rows, size)], sems.at[2 * i + j]
                    )
                )
        return out

    added = [pltpu.make_async_copy(extra[i], more.at[i], out_sems.at[len(pieces) + i]) for i in range(extras)]

    def run(size):
        copies = loads(size)
        for copy in copies + added:
            copy.start()
        stores = []
        for i, out in enumerate(outs):
            copies[2 * i].wait()
            copies[2 * i + 1].wait()
            last = extras and i == len(outs) - 1
            if last:
                for copy in added:
                    copy.wait()

            def chunk(c, _):
                here = pl.ds(pl.multiple_of(i * rows + c * CHUNK, CHUNK), CHUNK)
                there = pl.ds(pl.multiple_of(i * rows + half + c * CHUNK, CHUNK), CHUNK)
                if size == rows:
                    if not last:
                        sent[here, :] = kept[here, :] + came[here, :]
                        return 0
                    total = kept[here, :].astype(F32) + came[here, :].astype(F32)
                    total = total + more[0, pl.ds(pl.multiple_of(c * CHUNK, CHUNK), CHUNK), :].astype(F32)
                    sent[here, :] = total.astype(BF16)
                    return 0
                for source, target, offset in ((kept, here, 0), (came, there, half)):
                    value = source[here, :]
                    if last:
                        value = value + more[0, pl.ds(pl.multiple_of(offset + c * CHUNK, CHUNK), CHUNK), :]
                    sent[target, :] = value
                return 0

            lax.fori_loop(0, size // CHUNK, chunk, 0)
            store = pltpu.make_async_copy(sent.at[pl.ds(i * rows, rows)], out, out_sems.at[i])
            store.start()
            stores.append(store)
        for store in stores:
            store.wait()

    @pl.when(core == 0)
    def _():
        run(rows)

    @pl.when(core == 1)
    def _():
        run(half)


def join(keep, got, rows, pieces, extra=()):
    width = keep.shape[1]
    count = len(pieces)
    shape = jax.ShapeDtypeStruct((rows, width), BF16)
    return pl.pallas_call(
        lambda *refs: join_kernel(pieces, len(extra), *refs),
        out_shape=(shape,) * count,
        in_specs=[HBM] * (2 + len(extra)),
        out_specs=(HBM,) * count,
        scratch_shapes=[
            pltpu.VMEM((count * rows, width), BF16),
            pltpu.VMEM((count * rows, width), BF16),
            pltpu.VMEM((1, rows, width), BF16),
            pltpu.VMEM((count * rows, width), BF16),
            pltpu.SemaphoreType.DMA((2 * count,)),
            pltpu.SemaphoreType.DMA((count + 1,)),
        ],
        compiler_params=BIG,
        name="join",
    )(keep, got, *extra)


def each_chunk(rows, step):
    def run(c, _):
        step(pl.ds(pl.multiple_of(c * CHUNK, CHUNK), CHUNK), c)
        return 0

    lax.fori_loop(0, rows // CHUNK, run, 0)


def total_of(refs, part):
    total = refs[0][part, :].astype(F32)
    for ref in refs[1:]:
        total = total + ref[part, :].astype(F32)
    return total


def add_kernel(*refs):
    def step(part, c):
        refs[-1][part, :] = total_of(refs[:-1], part).astype(refs[-1].dtype)

    each_chunk(refs[-1].shape[0], step)


def add(*values):
    rows, width = values[0].shape
    block = pl.BlockSpec((rows // 2, width), lambda i: (i, 0))
    return pl.pallas_call(
        add_kernel,
        grid=(2,),
        out_shape=jax.ShapeDtypeStruct((rows, width), BF16),
        in_specs=[block] * len(values),
        out_specs=block,
        compiler_params=BIG,
        name="add",
    )(*values)


def split_kernel(*refs):
    half = refs[-1].shape[0]

    def step(part, c):
        refs[-2][part, :] = total_of(refs[:-2], part)
        other = pl.ds(pl.multiple_of(half + c * CHUNK, CHUNK), CHUNK)
        refs[-1][part, :] = total_of(refs[:-2], other)

    each_chunk(half, step)


def split_total(*values):
    shape = jax.ShapeDtypeStruct((values[0].shape[0] // 2, values[0].shape[1]), F32)
    return pl.pallas_call(
        split_kernel,
        out_shape=(shape, shape),
        in_specs=[VMEM] * len(values),
        out_specs=(VMEM, VMEM),
        compiler_params=BIG,
        name="split_total",
    )(*values)


def finish_kernel(scale, image, text, kept, got, far, last, got_far, got_last, image_grad, text_grad):
    core = lax.axis_index("col") % 2

    def backward(raw, parts):
        unit, inverse = normalize(raw[...])
        unit_grad = scale[0] * (parts[0][...] + parts[1][...].astype(F32) + parts[2][...].astype(F32))
        along = jnp.sum(unit * unit_grad, axis=1, keepdims=True)
        return inverse * (unit_grad - unit * along)

    @pl.when(core == 0)
    def _():
        image_grad[...] = backward(image, (kept, far, last))
        text_grad[...] = backward(text, (got, got_far, got_last))

    @pl.when(core == 1)
    def _():
        image_grad[...] = backward(image, (got, got_far, got_last))
        text_grad[...] = backward(text, (kept, far, last))


def finish(scale, image, text, kept, got, far, last):
    rows, width = image.shape
    shape = jax.ShapeDtypeStruct(image.shape, F32)
    block = pl.BlockSpec((rows // 2, width), lambda i: (i, 0))
    other = pl.BlockSpec((rows // 2, width), lambda i: (2 + i, 0))
    return pl.pallas_call(
        finish_kernel,
        grid=(2,),
        out_shape=(shape, shape),
        in_specs=[SMEM] + [block] * 6 + [other] * 2,
        out_specs=(block, block),
        compiler_params=BIG,
        name="finish",
    )(scale, image, text, kept, got, far, last, send(far, CORES), send(last, CORES))


def after(values, first):
    return lax.optimization_barrier((tuple(values), first))


def after(values, first):
    return list(lax.optimization_barrier((tuple(values), first))[0])


def shards(image, text, labels, sharpness, shift):
    scale = (sharpness, shift)
    rows = 2 * image.shape[0]
    own0 = prepare(image, text, labels)
    mate0 = send(own0, MATES)
    up, down, far = (send(own0, ring(-d)) for d in STEPS[1:])
    own = [own0, up, down, mate0]
    own_other = [send(piece, CORES) for piece in own]
    mate = [far] + [send(mate0, ring(-d)) for d in STEPS[1:3]] + [send(far, MATES)]
    before = own_sums(scale, own, own_other)
    mate = mate[:1] + after(mate[1:], before)
    mate_other = [send(piece, CORES) for piece in mate]
    keeps, aways = rest_sums(scale, own + mate, own_other + mate_other, before)

    gone = send(aways[0], CORES)
    own_gone, last_gone = (send(away, CORES) for away in after(aways[1:], gone))
    mate_up, mate_down, far = join(keeps[0], gone, rows, (0, 1, 2))
    far = send(far, MATES)
    mate_up, mate_down = send(mate_up, ring(1)), send(mate_down, ring(-1))
    up, down = join(keeps[1], own_gone, rows, (0, 1))
    up, down = send(up, ring(1)), send(down, ring(-1))
    (far,) = join(keeps[2], last_gone, rows, (1,), (far,))
    own_part, mate_part = join(keeps[2], last_gone, rows, (0, 2))
    (mate_part,) = after((mate_part,), far)
    far = send(far, ring(2))
    mate_total = send(add(mate_part, mate_up, mate_down), MATES)
    kept, away = split_total(own_part, up, down)
    return finish(sharpness, image, text, kept, send(away, CORES), far, mate_total)


def solution(mesh):
    spec = P(AXES, None)
    return jax.shard_map(
        shards,
        mesh=mesh,
        in_specs=(spec, spec, P(AXES), P(), P()),
        out_specs=(spec, spec),
        check_vma=False,
    )
```

```python
import jax
import jax.numpy as jnp
from jax import lax
from jax.experimental import pallas as pl
from jax.experimental.pallas import tpu as pltpu
from jax.sharding import PartitionSpec as P

AXES = ("row", "col")
VMEM = pl.BlockSpec(memory_space=pltpu.VMEM)
SMEM = pl.BlockSpec(memory_space=pltpu.SMEM)
HBM = pl.BlockSpec(memory_space=pltpu.HBM)
BIG = pltpu.CompilerParams(vmem_limit_bytes=64 * 2**20)
F32 = jnp.float32
BF16 = jnp.bfloat16


def device(x, y, z, k):
    return (y % 4 * 2 + z % 2) * 16 + x % 4 * 4 + z % 4 // 2 * 2 + k


def z_mate(z, k):
    return z + 1 if (z + k) % 2 == 0 else z - 1


def pairs(move):
    out = []
    for x in range(4):
        for y in range(4):
            for z in range(4):
                for k in range(2):
                    out.append((device(x, y, z, k), device(*move(x, y, z, k))))
    return out


def ring(step):
    return pairs(lambda x, y, z, k: (x + step, y, z, k) if k == 0 else (x, y + step, z, k))


CORES = pairs(lambda x, y, z, k: (x, y, z, 1 - k))
MATES = pairs(lambda x, y, z, k: (x, y, z_mate(z, k), k))
STEPS = (0, 1, -1, 2)
GROUPS = (((0, False), (1, False), (-1, False), (0, True)), ((2, False), (1, True), (-1, True), (2, True)))
CHUNK = 32


def send(value, perm):
    return lax.ppermute(value, AXES, perm)


def normalize(raw):
    values = raw.astype(F32)
    inverse = lax.rsqrt(jnp.sum(values * values, axis=1, keepdims=True) + 1e-06)
    return values * inverse, inverse


def whoami():
    row, col = lax.axis_index("row"), lax.axis_index("col")
    return col // 4, row // 2, col // 2 % 2 * 2 + row % 2, col % 2


def prepare_kernel(image, text, other_image, other_text, labels, other_labels, own):
    core = lax.axis_index("col") % 2
    rows = image.shape[0]

    def fill(mine, other):
        def step(part, c):
            own[part, :] = normalize(mine[part, :])[0].astype(BF16)
            own[pl.ds(pl.multiple_of(rows + c * CHUNK, CHUNK), CHUNK), :] = normalize(other[part, :])[0].astype(BF16)

        each_chunk(rows, step)

    @pl.when(core == 0)
    def _():
        fill(image, other_image)

    @pl.when(core == 1)
    def _():
        fill(text, other_text)

    line = lax.broadcasted_iota(jnp.int32, (16, rows), 0)
    digits = jnp.zeros((16, rows), F32)
    for k, label in enumerate((labels[...], other_labels[...])):
        high = lax.shift_right_logical(label, 8).astype(F32)
        low = jnp.bitwise_and(label, 255).astype(F32)
        digits = jnp.where(line == 2 * k, high, jnp.where(line == 2 * k + 1, low, digits))
    own[2 * rows :, :] = jnp.zeros((16, image.shape[1]), BF16)
    own[2 * rows :, :rows] = digits.astype(BF16)


def prepare(image, text, labels):
    rows, width = image.shape
    labels = labels.reshape(1, rows)
    return pl.pallas_call(
        prepare_kernel,
        out_shape=jax.ShapeDtypeStruct((2 * rows + 16, width), BF16),
        in_specs=[VMEM] * 6,
        out_specs=VMEM,
        compiler_params=BIG,
        name="prepare",
    )(image, text, send(image, CORES), send(text, CORES), labels, send(labels, CORES))


class Blocks:
    def __init__(self, mine, other, images, digits, texts, labels, sems):
        self.mine, self.other = mine, other
        self.images, self.digits, self.texts, self.labels, self.sems = images, digits, texts, labels, sems
        self.rows = mine[0].shape[0] - 16
        self.half = self.rows // 2
        self.pieces = len(mine)

    def copies(self, image_from, text_from, offset):
        rows, half = self.rows, self.half
        text, image = [], []
        for p in range(self.pieces):
            text.append((text_from[p].at[pl.ds(offset, half)], self.texts.at[pl.ds(p * half, half)]))
            image.append((image_from[p].at[pl.ds(0, rows)], self.images.at[pl.ds(p * rows, rows)]))
            image.append((image_from[p].at[pl.ds(rows, 16)], self.digits.at[p]))
        return [(a, b, self.sems.at[i]) for i, (a, b) in enumerate(text + image)]

    def each(self, core, wait, which):
        part = {"text": slice(0, self.pieces), "image": slice(self.pieces, None)}[which]

        def act(copies):
            for copy in copies[part]:
                copy = pltpu.make_async_copy(*copy)
                copy.wait() if wait else copy.start()

        @pl.when(core == 0)
        def _():
            act(self.copies(self.mine, self.other, self.half))

        @pl.when(core == 1)
        def _():
            act(self.copies(self.other, self.mine, 0))

    def set_labels(self):
        for p in range(self.pieces):
            digit = self.digits[p].astype(F32)
            for k in range(2):
                number = digit[2 * k : 2 * k + 1, : self.half] * 256.0 + digit[2 * k + 1 : 2 * k + 2, : self.half]
                start = p * self.rows + k * self.half
                self.labels[:, start : start + self.half] = jnp.broadcast_to(number, (8, self.half))


def set_coefficient(scale, late, texts, images, labels, out):
    a, b = 0.5 * scale[0][0], 0.5 * scale[1][0]
    half = texts.shape[0] // 4
    x, y, z, core = whoami()
    mate_z = jnp.where(z % 2 == 1, z + 1, z + 3) % 4
    logits = lax.dot_general(texts[...], images[...], (((1,), (1,)), ((), ())), preferred_element_type=F32)
    label = labels[0:1, :]
    position = lax.broadcasted_iota(jnp.int32, (half, label.shape[1]), 0).astype(F32)
    for p in range(4):
        (near_step, near_mate), (far_step, far_mate) = GROUPS[0][p], GROUPS[1][p]
        one = device_at(x, y + near_step + 4, mate_z if near_mate else z, core)
        two = device_at(x, y + far_step + 4, mate_z if far_mate else z, core)
        first = (jnp.where(late, two, one) * half).astype(F32)
        part = slice(p * half, (p + 1) * half)
        shift = jnp.where(position == label - first, -0.5, 0.5)
        out[part, :] = (0.5 * jnp.tanh(logits[part, :] * a + b) + shift).astype(BF16)


def device_at(x, y, z, k):
    return (y % 4 * 2 + z % 2) * 16 + x * 4 + z // 2 * 2 + k


def along_text(coefficient, images):
    return jnp.dot(coefficient[...], images[...], preferred_element_type=F32)


def along_image(coefficient, texts):
    return lax.dot_general(coefficient[...], texts[...], (((0,), (0,)), ((), ())), preferred_element_type=F32)


def own_kernel(sharpness, shift, *refs):
    mine, other = refs[:4], refs[4:8]
    image_to, text_to = refs[8:10]
    images, digits, labels, texts, coefficient, image_sum, text_sum, sems, out_sem = refs[10:]
    core = lax.axis_index("col") % 2
    group = Blocks(mine, other, images, digits, texts, labels, sems)
    for wait in (False, True):
        group.each(core, wait, "text")
        group.each(core, wait, "image")
    group.set_labels()
    set_coefficient((sharpness, shift), False, texts, images, labels, coefficient)
    text_sum[...] = along_text(coefficient, images)
    copies = [pltpu.make_async_copy(text_sum, text_to, out_sem.at[0])]
    copies[0].start()
    part = images.shape[0] // 2
    for i in range(2):
        here = pl.ds(i * part, part)
        image_sum[here, :] = along_image(coefficient.at[:, here], texts)
        copies.append(pltpu.make_async_copy(image_sum.at[here], image_to.at[here], out_sem.at[1 + i]))
        copies[-1].start()
    for copy in copies:
        copy.wait()


def group_scratch(rows, width):
    return [
        pltpu.VMEM((4 * rows, width), BF16),
        pltpu.VMEM((4, 16, width), BF16),
        pltpu.VMEM((8, 4 * rows), F32),
    ]


def cost(quads, rows, width):
    flops = quads * 6 * 8 * rows * rows * width
    return pl.CostEstimate(flops=flops, bytes_accessed=quads * 20 * rows * width, transcendentals=quads * 8 * rows * rows)


def own_sums(scale, mine, other):
    rows, width = mine[0].shape[0] - 16, mine[0].shape[1]
    return pl.pallas_call(
        own_kernel,
        out_shape=(jax.ShapeDtypeStruct((4 * rows, width), F32), jax.ShapeDtypeStruct((2 * rows, width), F32)),
        in_specs=[SMEM] * 2 + [HBM] * 8,
        out_specs=(HBM, HBM),
        scratch_shapes=group_scratch(rows, width)
        + [
            pltpu.VMEM((2 * rows, width), BF16),
            pltpu.VMEM((2 * rows, 4 * rows), BF16),
            pltpu.VMEM((4 * rows, width), F32),
            pltpu.VMEM((2 * rows, width), F32),
            pltpu.SemaphoreType.DMA((12,)),
            pltpu.SemaphoreType.DMA((3,)),
        ],
        compiler_params=BIG,
        cost_estimate=cost(1, rows, width),
        name="own_sums",
    )(*scale, *mine, *other)


LEAVING = (((1, 1, 1), (1, 2, 2)), ((0, 1, 2),), ((0, 0, 1), (1, 0, 1), (0, 3, 1)))


def rest_kernel(sharpness, shift, *refs):
    scale = (sharpness, shift)
    own_mine, mate_mine, own_other, mate_other = refs[:4], refs[4:8], refs[8:12], refs[12:16]
    image_before, text_before = refs[16:18]
    keeps, aways = refs[18:21], refs[21:24]
    images, digits, labels, texts, image_total, text_total, coefficient, image_out, text_out = refs[24:33]
    sems, before_sem, out_sem = refs[33:]
    core = lax.axis_index("col") % 2
    rows = own_mine[0].shape[0] - 16
    half = rows // 2
    own = Blocks(own_mine, own_other, images.at[0], digits.at[0], texts.at[0], labels.at[0], sems.at[0])
    mate = Blocks(mate_mine, mate_other, images.at[1], digits.at[1], texts.at[1], labels.at[1], sems.at[1])
    before = [
        pltpu.make_async_copy(image_before, image_total.at[0], before_sem.at[0]),
        pltpu.make_async_copy(text_before, text_total.at[0], before_sem.at[1]),
    ]
    mate.each(core, False, "text")
    own.each(core, False, "image")
    image_total[1] = jnp.zeros_like(image_total[1])
    text_total[1] = jnp.zeros_like(text_total[1])

    def flush(wait, wanted):
        def act(image_to, text_to):
            sem = 0
            for g, spans in enumerate(LEAVING):
                at = 0
                for group, first, count in spans:
                    for kind, source, target, size in (
                        (0, image_out, image_to[g], rows),
                        (1, text_out, text_to[g], half),
                    ):
                        if not wanted(kind, group, first):
                            sem += 1
                            continue
                        copy = pltpu.make_async_copy(
                            source.at[group, pl.ds(first * size, count * size)],
                            target.at[pl.ds(at * size, count * size)],
                            out_sem.at[sem],
                        )
                        copy.wait() if wait else copy.start()
                        sem += 1
                    at += count

        @pl.when(core == 0)
        def _():
            act(keeps, aways)

        @pl.when(core == 1)
        def _():
            act(aways, keeps)

    def block(q, _):
        i = jnp.minimum(q, 1)
        t = 1 - q % 2

        @pl.when(q == 0)
        def _():
            mate.each(core, True, "text")
            own.each(core, True, "image")
            before[0].start()
            own.each(core, False, "text")
            mate.each(core, False, "image")
            before[1].start()
            own.set_labels()

        @pl.when(q == 1)
        def _():
            own.each(core, True, "text")
            mate.each(core, True, "image")
            mate.set_labels()
            before[1].wait()

        set_coefficient(scale, t == 1, texts.at[t], images.at[i], labels.at[i], coefficient)
        text_sum = text_total[t] + along_text(coefficient, images.at[i])
        text_total[t] = text_sum
        text_out[t] = text_sum.astype(BF16)

        @pl.when(q == 0)
        def _():
            before[0].wait()

        @pl.when(q == 1)
        def _():
            flush(False, lambda kind, group, first: kind == 1 and group == 0)

        @pl.when(q == 2)
        def _():
            flush(False, lambda kind, group, first: kind == 1 and group == 1)

        for h in range(2):
            here = pl.ds(2 * h * rows, 2 * rows)
            image_sum = image_total[i, here, :] + along_image(coefficient.at[:, here], texts.at[t])
            image_total[i, here, :] = image_sum
            image_out[i, here, :] = image_sum.astype(BF16)

            if h == 0:

                @pl.when(q == 2)
                def _():
                    flush(False, lambda kind, group, first: kind == 0 and group == 1 and first < 2)

        @pl.when(q == 0)
        def _():
            flush(False, lambda kind, group, first: kind == 0 and group == 0)

        return 0

    lax.fori_loop(0, 3, block, 0)
    flush(False, lambda kind, group, first: kind == 0 and group == 1 and first >= 2)
    flush(True, lambda kind, group, first: True)


def rest_sums(scale, mine, other, before):
    rows, width = mine[0].shape[0] - 16, mine[0].shape[1]
    shapes = [jax.ShapeDtypeStruct((sum(n for _, _, n in spans) * rows, width), BF16) for spans in LEAVING]
    outs = pl.pallas_call(
        rest_kernel,
        out_shape=tuple(shapes * 2),
        in_specs=[SMEM] * 2 + [HBM] * 18,
        out_specs=(HBM,) * 6,
        scratch_shapes=[
            pltpu.VMEM((2, 4 * rows, width), BF16),
            pltpu.VMEM((2, 4, 16, width), BF16),
            pltpu.VMEM((2, 8, 4 * rows), F32),
            pltpu.VMEM((2, 2 * rows, width), BF16),
            pltpu.VMEM((2, 4 * rows, width), F32),
            pltpu.VMEM((2, 2 * rows, width), F32),
            pltpu.VMEM((2 * rows, 4 * rows), BF16),
            pltpu.VMEM((2, 4 * rows, width), BF16),
            pltpu.VMEM((2, 2 * rows, width), BF16),
            pltpu.SemaphoreType.DMA((2, 12)),
            pltpu.SemaphoreType.DMA((2,)),
            pltpu.SemaphoreType.DMA((12,)),
        ],
        compiler_params=BIG,
        cost_estimate=cost(3, rows, width),
        name="rest_sums",
    )(*scale, *mine, *other, *before)
    return outs[:3], outs[3:]


def join_kernel(pieces, extras, keep, got, *refs):
    extra, outs = refs[:extras], refs[extras : extras + len(pieces)]
    kept, came, more, sent, sems, out_sems = refs[extras + len(pieces) :]
    core = lax.axis_index("col") % 2
    rows = outs[0].shape[0]
    half = rows // 2

    def loads(size):
        out = []
        for i, p in enumerate(pieces):
            for j, (a, b) in enumerate(((keep, kept), (got, came))):
                out.append(
                    pltpu.make_async_copy(
                        a.at[pl.ds(p * size, size)], b.at[pl.ds(i * rows, size)], sems.at[2 * i + j]
                    )
                )
        return out

    added = [pltpu.make_async_copy(extra[i], more.at[i], out_sems.at[len(pieces) + i]) for i in range(extras)]

    def run(size):
        copies = loads(size)
        for copy in copies + added:
            copy.start()
        stores = []
        for i, out in enumerate(outs):
            copies[2 * i].wait()
            copies[2 * i + 1].wait()
            last = extras and i == len(outs) - 1
            if last:
                for copy in added:
                    copy.wait()

            def chunk(c, _):
                here = pl.ds(pl.multiple_of(i * rows + c * CHUNK, CHUNK), CHUNK)
                there = pl.ds(pl.multiple_of(i * rows + half + c * CHUNK, CHUNK), CHUNK)
                if size == rows:
                    if not last:
                        sent[here, :] = kept[here, :] + came[here, :]
                        return 0
                    total = kept[here, :].astype(F32) + came[here, :].astype(F32)
                    total = total + more[0, pl.ds(pl.multiple_of(c * CHUNK, CHUNK), CHUNK), :].astype(F32)
                    sent[here, :] = total.astype(BF16)
                    return 0
                for source, target, offset in ((kept, here, 0), (came, there, half)):
                    value = source[here, :]
                    if last:
                        value = value + more[0, pl.ds(pl.multiple_of(offset + c * CHUNK, CHUNK), CHUNK), :]
                    sent[target, :] = value
                return 0

            lax.fori_loop(0, size // CHUNK, chunk, 0)
            store = pltpu.make_async_copy(sent.at[pl.ds(i * rows, rows)], out, out_sems.at[i])
            store.start()
            stores.append(store)
        for store in stores:
            store.wait()

    @pl.when(core == 0)
    def _():
        run(rows)

    @pl.when(core == 1)
    def _():
        run(half)


def join(keep, got, rows, pieces, extra=()):
    width = keep.shape[1]
    count = len(pieces)
    shape = jax.ShapeDtypeStruct((rows, width), BF16)
    return pl.pallas_call(
        lambda *refs: join_kernel(pieces, len(extra), *refs),
        out_shape=(shape,) * count,
        in_specs=[HBM] * (2 + len(extra)),
        out_specs=(HBM,) * count,
        scratch_shapes=[
            pltpu.VMEM((count * rows, width), BF16),
            pltpu.VMEM((count * rows, width), BF16),
            pltpu.VMEM((1, rows, width), BF16),
            pltpu.VMEM((count * rows, width), BF16),
            pltpu.SemaphoreType.DMA((2 * count,)),
            pltpu.SemaphoreType.DMA((count + 1,)),
        ],
        compiler_params=BIG,
        name="join",
    )(keep, got, *extra)


def each_chunk(rows, step, size=CHUNK):
    def run(c, _):
        step(pl.ds(pl.multiple_of(c * size, size), size), c)
        return 0

    lax.fori_loop(0, rows // size, run, 0)


def total_of(refs, part):
    total = refs[0][part, :].astype(F32)
    for ref in refs[1:]:
        total = total + ref[part, :].astype(F32)
    return total


def add_kernel(*refs):
    def step(part, c):
        refs[-1][part, :] = total_of(refs[:-1], part).astype(refs[-1].dtype)

    each_chunk(refs[-1].shape[0], step)


def add(*values):
    rows, width = values[0].shape
    block = pl.BlockSpec((rows // 2, width), lambda i: (i, 0))
    return pl.pallas_call(
        add_kernel,
        grid=(2,),
        out_shape=jax.ShapeDtypeStruct((rows, width), BF16),
        in_specs=[block] * len(values),
        out_specs=block,
        compiler_params=BIG,
        name="add",
    )(*values)


def split_kernel(*refs):
    half = refs[-1].shape[0]

    def step(part, c):
        refs[-2][part, :] = total_of(refs[:-2], part)
        other = pl.ds(pl.multiple_of(half + c * CHUNK, CHUNK), CHUNK)
        refs[-1][part, :] = total_of(refs[:-2], other)

    each_chunk(half, step)


def split_total(*values):
    shape = jax.ShapeDtypeStruct((values[0].shape[0] // 2, values[0].shape[1]), F32)
    return pl.pallas_call(
        split_kernel,
        out_shape=(shape, shape),
        in_specs=[VMEM] * len(values),
        out_specs=(VMEM, VMEM),
        compiler_params=BIG,
        name="split_total",
    )(*values)


def finish_kernel(scale, image, text, kept, got, far, last, got_far, got_last, image_grad, text_grad):
    core = lax.axis_index("col") % 2

    def backward(raw, parts, out):
        def step(part, c):
            unit, inverse = normalize(raw[part, :])
            total = parts[0][part, :] + parts[1][part, :].astype(F32) + parts[2][part, :].astype(F32)
            unit_grad = scale[0] * total
            along = jnp.sum(unit * unit_grad, axis=1, keepdims=True)
            out[part, :] = inverse * (unit_grad - unit * along)

        each_chunk(out.shape[0], step, 16)

    @pl.when(core == 0)
    def _():
        backward(image, (kept, far, last), image_grad)
        backward(text, (got, got_far, got_last), text_grad)

    @pl.when(core == 1)
    def _():
        backward(image, (got, got_far, got_last), image_grad)
        backward(text, (kept, far, last), text_grad)


def finish(scale, image, text, kept, got, far, last):
    rows, width = image.shape
    shape = jax.ShapeDtypeStruct(image.shape, F32)
    block = pl.BlockSpec((rows // 2, width), lambda i: (i, 0))
    other = pl.BlockSpec((rows // 2, width), lambda i: (2 + i, 0))
    return pl.pallas_call(
        finish_kernel,
        grid=(2,),
        out_shape=(shape, shape),
        in_specs=[SMEM] + [block] * 6 + [other] * 2,
        out_specs=(block, block),
        compiler_params=BIG,
        name="finish",
    )(scale, image, text, kept, got, far, last, send(far, CORES), send(last, CORES))


def after(values, first):
    return lax.optimization_barrier((tuple(values), first))


def after(values, first):
    return list(lax.optimization_barrier((tuple(values), first))[0])


def shards(image, text, labels, sharpness, shift):
    scale = (sharpness, shift)
    rows = 2 * image.shape[0]
    own0 = prepare(image, text, labels)
    mate0 = send(own0, MATES)
    up, down, far = (send(own0, ring(-d)) for d in STEPS[1:])
    own = [own0, up, down, mate0]
    own_other = [send(piece, CORES) for piece in own]
    mate = [far] + [send(mate0, ring(-d)) for d in STEPS[1:3]] + [send(far, MATES)]
    before = own_sums(scale, own, own_other)
    mate = mate[:1] + after(mate[1:], before)
    mate_other = [send(piece, CORES) for piece in mate]
    keeps, aways = rest_sums(scale, own + mate, own_other + mate_other, before)

    gone = send(aways[0], CORES)
    own_gone, last_gone = (send(away, CORES) for away in after(aways[1:], gone))
    mate_up, mate_down, far = join(keeps[0], gone, rows, (0, 1, 2))
    far = send(far, MATES)
    mate_up, mate_down = send(mate_up, ring(1)), send(mate_down, ring(-1))
    up, down = join(keeps[1], own_gone, rows, (0, 1))
    up, down = send(up, ring(1)), send(down, ring(-1))
    (far,) = join(keeps[2], last_gone, rows, (1,), (far,))
    own_part, mate_part = join(keeps[2], last_gone, rows, (0, 2))
    (mate_part,) = after((mate_part,), far)
    far = send(far, ring(2))
    mate_total = send(add(mate_part, mate_up, mate_down), MATES)
    kept, away = split_total(own_part, up, down)
    return finish(sharpness, image, text, kept, send(away, CORES), far, mate_total)


def solution(mesh):
    spec = P(AXES, None)
    return jax.shard_map(
        shards,
        mesh=mesh,
        in_specs=(spec, spec, P(AXES), P(), P()),
        out_specs=(spec, spec),
        check_vma=False,
    )
```

```python
import jax
import jax.numpy as jnp
from jax import lax
from jax.experimental import pallas as pl
from jax.experimental.pallas import tpu as pltpu
from jax.sharding import PartitionSpec as P

AXES = ("row", "col")
VMEM = pl.BlockSpec(memory_space=pltpu.VMEM)
SMEM = pl.BlockSpec(memory_space=pltpu.SMEM)
HBM = pl.BlockSpec(memory_space=pltpu.HBM)
BIG = pltpu.CompilerParams(vmem_limit_bytes=64 * 2**20)
F32 = jnp.float32
BF16 = jnp.bfloat16


def device(x, y, z, k):
    return (y % 4 * 2 + z % 2) * 16 + x % 4 * 4 + z % 4 // 2 * 2 + k


def z_mate(z, k):
    return z + 1 if (z + k) % 2 == 0 else z - 1


def pairs(move):
    out = []
    for x in range(4):
        for y in range(4):
            for z in range(4):
                for k in range(2):
                    out.append((device(x, y, z, k), device(*move(x, y, z, k))))
    return out


def ring(step):
    return pairs(lambda x, y, z, k: (x + step, y, z, k) if k == 0 else (x, y + step, z, k))


CORES = pairs(lambda x, y, z, k: (x, y, z, 1 - k))
MATES = pairs(lambda x, y, z, k: (x, y, z_mate(z, k), k))
STEPS = (0, 1, -1, 2)
GROUPS = (((0, False), (1, False), (-1, False), (0, True)), ((2, False), (1, True), (-1, True), (2, True)))
CHUNK = 32


def send(value, perm):
    return lax.ppermute(value, AXES, perm)


def normalize(raw):
    values = raw.astype(F32)
    inverse = lax.rsqrt(jnp.sum(values * values, axis=1, keepdims=True) + 1e-06)
    return values * inverse, inverse


def whoami():
    row, col = lax.axis_index("row"), lax.axis_index("col")
    return col // 4, row // 2, col // 2 % 2 * 2 + row % 2, col % 2


def prepare_kernel(image, text, other_image, other_text, labels, other_labels, own):
    core = lax.axis_index("col") % 2
    rows = image.shape[0]

    def fill(mine, other):
        own[:rows, :] = normalize(mine[...])[0].astype(BF16)
        own[rows : 2 * rows, :] = normalize(other[...])[0].astype(BF16)

    @pl.when(core == 0)
    def _():
        fill(image, other_image)

    @pl.when(core == 1)
    def _():
        fill(text, other_text)

    line = lax.broadcasted_iota(jnp.int32, (16, rows), 0)
    digits = jnp.zeros((16, rows), F32)
    for k, label in enumerate((labels[...], other_labels[...])):
        high = lax.shift_right_logical(label, 8).astype(F32)
        low = jnp.bitwise_and(label, 255).astype(F32)
        digits = jnp.where(line == 2 * k, high, jnp.where(line == 2 * k + 1, low, digits))
    own[2 * rows :, :] = jnp.zeros((16, image.shape[1]), BF16)
    own[2 * rows :, :rows] = digits.astype(BF16)


def prepare(image, text, labels):
    rows, width = image.shape
    labels = labels.reshape(1, rows)
    return pl.pallas_call(
        prepare_kernel,
        out_shape=jax.ShapeDtypeStruct((2 * rows + 16, width), BF16),
        in_specs=[VMEM] * 6,
        out_specs=VMEM,
        compiler_params=BIG,
        name="prepare",
    )(image, text, send(image, CORES), send(text, CORES), labels, send(labels, CORES))


class Blocks:
    def __init__(self, mine, other, images, digits, texts, labels, sems):
        self.mine, self.other = mine, other
        self.images, self.digits, self.texts, self.labels, self.sems = images, digits, texts, labels, sems
        self.rows = mine[0].shape[0] - 16
        self.half = self.rows // 2
        self.pieces = len(mine)

    def copies(self, image_from, text_from, offset):
        rows, half = self.rows, self.half
        text, image = [], []
        for p in range(self.pieces):
            text.append((text_from[p].at[pl.ds(offset, half)], self.texts.at[pl.ds(p * half, half)]))
            image.append((image_from[p].at[pl.ds(0, rows)], self.images.at[pl.ds(p * rows, rows)]))
            image.append((image_from[p].at[pl.ds(rows, 16)], self.digits.at[p]))
        return [(a, b, self.sems.at[i]) for i, (a, b) in enumerate(text + image)]

    def each(self, core, wait, which):
        part = {"text": slice(0, self.pieces), "image": slice(self.pieces, None)}[which]

        def act(copies):
            for copy in copies[part]:
                copy = pltpu.make_async_copy(*copy)
                copy.wait() if wait else copy.start()

        @pl.when(core == 0)
        def _():
            act(self.copies(self.mine, self.other, self.half))

        @pl.when(core == 1)
        def _():
            act(self.copies(self.other, self.mine, 0))

    def set_labels(self):
        for p in range(self.pieces):
            digit = self.digits[p].astype(F32)
            for k in range(2):
                number = digit[2 * k : 2 * k + 1, : self.half] * 256.0 + digit[2 * k + 1 : 2 * k + 2, : self.half]
                start = p * self.rows + k * self.half
                self.labels[:, start : start + self.half] = jnp.broadcast_to(number, (8, self.half))


def set_coefficient(scale, late, texts, images, labels, out):
    a, b = 0.5 * scale[0][0], 0.5 * scale[1][0]
    half = texts.shape[0] // 4
    x, y, z, core = whoami()
    mate_z = jnp.where(z % 2 == 1, z + 1, z + 3) % 4
    logits = lax.dot_general(texts[...], images[...], (((1,), (1,)), ((), ())), preferred_element_type=F32)
    label = labels[0:1, :]
    position = lax.broadcasted_iota(jnp.int32, (half, label.shape[1]), 0).astype(F32)
    for p in range(4):
        (near_step, near_mate), (far_step, far_mate) = GROUPS[0][p], GROUPS[1][p]
        one = device_at(x, y + near_step + 4, mate_z if near_mate else z, core)
        two = device_at(x, y + far_step + 4, mate_z if far_mate else z, core)
        first = (jnp.where(late, two, one) * half).astype(F32)
        part = slice(p * half, (p + 1) * half)
        shift = jnp.where(position == label - first, -0.5, 0.5)
        out[part, :] = (0.5 * jnp.tanh(logits[part, :] * a + b) + shift).astype(BF16)


def device_at(x, y, z, k):
    return (y % 4 * 2 + z % 2) * 16 + x * 4 + z // 2 * 2 + k


def along_text(coefficient, images):
    return jnp.dot(coefficient[...], images[...], preferred_element_type=F32)


def along_image(coefficient, texts):
    return lax.dot_general(coefficient[...], texts[...], (((0,), (0,)), ((), ())), preferred_element_type=F32)


def own_kernel(sharpness, shift, *refs):
    mine, other = refs[:4], refs[4:8]
    image_to, text_to = refs[8:10]
    images, digits, labels, texts, coefficient, image_sum, text_sum, sems, out_sem = refs[10:]
    core = lax.axis_index("col") % 2
    group = Blocks(mine, other, images, digits, texts, labels, sems)
    for wait in (False, True):
        group.each(core, wait, "text")
        group.each(core, wait, "image")
    group.set_labels()
    set_coefficient((sharpness, shift), False, texts, images, labels, coefficient)
    text_sum[...] = along_text(coefficient, images)
    copies = [pltpu.make_async_copy(text_sum, text_to, out_sem.at[0])]
    copies[0].start()
    part = images.shape[0] * 7 // 10
    for i, here in enumerate((pl.ds(0, part), pl.ds(part, images.shape[0] - part))):
        image_sum[here, :] = along_image(coefficient.at[:, here], texts)
        copies.append(pltpu.make_async_copy(image_sum.at[here], image_to.at[here], out_sem.at[1 + i]))
        copies[-1].start()
    for copy in copies:
        copy.wait()


def group_scratch(rows, width):
    return [
        pltpu.VMEM((4 * rows, width), BF16),
        pltpu.VMEM((4, 16, width), BF16),
        pltpu.VMEM((8, 4 * rows), F32),
    ]


def cost(quads, rows, width):
    flops = quads * 6 * 8 * rows * rows * width
    return pl.CostEstimate(flops=flops, bytes_accessed=quads * 20 * rows * width, transcendentals=quads * 8 * rows * rows)


def own_sums(scale, mine, other):
    rows, width = mine[0].shape[0] - 16, mine[0].shape[1]
    return pl.pallas_call(
        own_kernel,
        out_shape=(jax.ShapeDtypeStruct((4 * rows, width), F32), jax.ShapeDtypeStruct((2 * rows, width), F32)),
        in_specs=[SMEM] * 2 + [HBM] * 8,
        out_specs=(HBM, HBM),
        scratch_shapes=group_scratch(rows, width)
        + [
            pltpu.VMEM((2 * rows, width), BF16),
            pltpu.VMEM((2 * rows, 4 * rows), BF16),
            pltpu.VMEM((4 * rows, width), F32),
            pltpu.VMEM((2 * rows, width), F32),
            pltpu.SemaphoreType.DMA((12,)),
            pltpu.SemaphoreType.DMA((3,)),
        ],
        compiler_params=BIG,
        cost_estimate=cost(1, rows, width),
        name="own_sums",
    )(*scale, *mine, *other)


LEAVING = (((1, 1, 1), (1, 2, 2)), ((0, 1, 2),), ((0, 0, 1), (1, 0, 1), (0, 3, 1)))


def rest_kernel(sharpness, shift, *refs):
    scale = (sharpness, shift)
    own_mine, mate_mine, own_other, mate_other = refs[:4], refs[4:8], refs[8:12], refs[12:16]
    image_before, text_before = refs[16:18]
    keeps, aways = refs[18:21], refs[21:24]
    images, digits, labels, texts, image_total, text_total, coefficient, image_out, text_out = refs[24:33]
    sems, before_sem, out_sem = refs[33:]
    core = lax.axis_index("col") % 2
    rows = own_mine[0].shape[0] - 16
    half = rows // 2
    own = Blocks(own_mine, own_other, images.at[0], digits.at[0], texts.at[0], labels.at[0], sems.at[0])
    mate = Blocks(mate_mine, mate_other, images.at[1], digits.at[1], texts.at[1], labels.at[1], sems.at[1])
    before = [
        pltpu.make_async_copy(image_before, image_total.at[0], before_sem.at[0]),
        pltpu.make_async_copy(text_before, text_total.at[0], before_sem.at[1]),
    ]
    mate.each(core, False, "text")
    own.each(core, False, "image")
    image_total[1] = jnp.zeros_like(image_total[1])
    text_total[1] = jnp.zeros_like(text_total[1])

    def flush(wait, wanted):
        def act(image_to, text_to):
            sem = 0
            for g, spans in enumerate(LEAVING):
                at = 0
                for group, first, count in spans:
                    for kind, source, target, size in (
                        (0, image_out, image_to[g], rows),
                        (1, text_out, text_to[g], half),
                    ):
                        if not wanted(kind, group, first):
                            sem += 1
                            continue
                        copy = pltpu.make_async_copy(
                            source.at[group, pl.ds(first * size, count * size)],
                            target.at[pl.ds(at * size, count * size)],
                            out_sem.at[sem],
                        )
                        copy.wait() if wait else copy.start()
                        sem += 1
                    at += count

        @pl.when(core == 0)
        def _():
            act(keeps, aways)

        @pl.when(core == 1)
        def _():
            act(aways, keeps)

    def block(q, _):
        i = jnp.minimum(q, 1)
        t = 1 - q % 2

        @pl.when(q == 0)
        def _():
            mate.each(core, True, "text")
            own.each(core, True, "image")
            before[0].start()
            own.each(core, False, "text")
            mate.each(core, False, "image")
            before[1].start()
            own.set_labels()

        @pl.when(q == 1)
        def _():
            own.each(core, True, "text")
            mate.each(core, True, "image")
            mate.set_labels()
            before[1].wait()

        set_coefficient(scale, t == 1, texts.at[t], images.at[i], labels.at[i], coefficient)
        text_sum = text_total[t] + along_text(coefficient, images.at[i])
        text_total[t] = text_sum
        text_out[t] = text_sum.astype(BF16)

        @pl.when(q == 0)
        def _():
            before[0].wait()

        @pl.when(q == 1)
        def _():
            flush(False, lambda kind, group, first: kind == 1 and group == 0)

        @pl.when(q == 2)
        def _():
            flush(False, lambda kind, group, first: kind == 1 and group == 1)

        for h in range(2):
            here = pl.ds(2 * h * rows, 2 * rows)
            image_sum = image_total[i, here, :] + along_image(coefficient.at[:, here], texts.at[t])
            image_total[i, here, :] = image_sum
            image_out[i, here, :] = image_sum.astype(BF16)

            if h == 0:

                @pl.when(q == 2)
                def _():
                    flush(False, lambda kind, group, first: kind == 0 and group == 1 and first < 2)

        @pl.when(q == 0)
        def _():
            flush(False, lambda kind, group, first: kind == 0 and group == 0)

        return 0

    lax.fori_loop(0, 3, block, 0)
    flush(False, lambda kind, group, first: kind == 0 and group == 1 and first >= 2)
    flush(True, lambda kind, group, first: True)


def rest_sums(scale, mine, other, before):
    rows, width = mine[0].shape[0] - 16, mine[0].shape[1]
    shapes = [jax.ShapeDtypeStruct((sum(n for _, _, n in spans) * rows, width), BF16) for spans in LEAVING]
    outs = pl.pallas_call(
        rest_kernel,
        out_shape=tuple(shapes * 2),
        in_specs=[SMEM] * 2 + [HBM] * 18,
        out_specs=(HBM,) * 6,
        scratch_shapes=[
            pltpu.VMEM((2, 4 * rows, width), BF16),
            pltpu.VMEM((2, 4, 16, width), BF16),
            pltpu.VMEM((2, 8, 4 * rows), F32),
            pltpu.VMEM((2, 2 * rows, width), BF16),
            pltpu.VMEM((2, 4 * rows, width), F32),
            pltpu.VMEM((2, 2 * rows, width), F32),
            pltpu.VMEM((2 * rows, 4 * rows), BF16),
            pltpu.VMEM((2, 4 * rows, width), BF16),
            pltpu.VMEM((2, 2 * rows, width), BF16),
            pltpu.SemaphoreType.DMA((2, 12)),
            pltpu.SemaphoreType.DMA((2,)),
            pltpu.SemaphoreType.DMA((12,)),
        ],
        compiler_params=BIG,
        cost_estimate=cost(3, rows, width),
        name="rest_sums",
    )(*scale, *mine, *other, *before)
    return outs[:3], outs[3:]


def join_kernel(pieces, extras, keep, got, *refs):
    extra, outs = refs[:extras], refs[extras : extras + len(pieces)]
    kept, came, more, sent, sems, out_sems = refs[extras + len(pieces) :]
    core = lax.axis_index("col") % 2
    rows = outs[0].shape[0]
    half = rows // 2

    def loads(size):
        out = []
        for i, p in enumerate(pieces):
            for j, (a, b) in enumerate(((keep, kept), (got, came))):
                out.append(
                    pltpu.make_async_copy(
                        a.at[pl.ds(p * size, size)], b.at[pl.ds(i * rows, size)], sems.at[2 * i + j]
                    )
                )
        return out

    added = [pltpu.make_async_copy(extra[i], more.at[i], out_sems.at[len(pieces) + i]) for i in range(extras)]

    def run(size):
        copies = loads(size)
        for copy in copies + added:
            copy.start()
        stores = []
        for i, out in enumerate(outs):
            copies[2 * i].wait()
            copies[2 * i + 1].wait()
            last = extras and i == len(outs) - 1
            if last:
                for copy in added:
                    copy.wait()

            def chunk(c, _):
                here = pl.ds(pl.multiple_of(i * rows + c * CHUNK, CHUNK), CHUNK)
                there = pl.ds(pl.multiple_of(i * rows + half + c * CHUNK, CHUNK), CHUNK)
                if size == rows:
                    if not last:
                        sent[here, :] = kept[here, :] + came[here, :]
                        return 0
                    total = kept[here, :].astype(F32) + came[here, :].astype(F32)
                    total = total + more[0, pl.ds(pl.multiple_of(c * CHUNK, CHUNK), CHUNK), :].astype(F32)
                    sent[here, :] = total.astype(BF16)
                    return 0
                for source, target, offset in ((kept, here, 0), (came, there, half)):
                    value = source[here, :]
                    if last:
                        value = value + more[0, pl.ds(pl.multiple_of(offset + c * CHUNK, CHUNK), CHUNK), :]
                    sent[target, :] = value
                return 0

            lax.fori_loop(0, size // CHUNK, chunk, 0)
            store = pltpu.make_async_copy(sent.at[pl.ds(i * rows, rows)], out, out_sems.at[i])
            store.start()
            stores.append(store)
        for store in stores:
            store.wait()

    @pl.when(core == 0)
    def _():
        run(rows)

    @pl.when(core == 1)
    def _():
        run(half)


def join(keep, got, rows, pieces, extra=()):
    width = keep.shape[1]
    count = len(pieces)
    shape = jax.ShapeDtypeStruct((rows, width), BF16)
    return pl.pallas_call(
        lambda *refs: join_kernel(pieces, len(extra), *refs),
        out_shape=(shape,) * count,
        in_specs=[HBM] * (2 + len(extra)),
        out_specs=(HBM,) * count,
        scratch_shapes=[
            pltpu.VMEM((count * rows, width), BF16),
            pltpu.VMEM((count * rows, width), BF16),
            pltpu.VMEM((1, rows, width), BF16),
            pltpu.VMEM((count * rows, width), BF16),
            pltpu.SemaphoreType.DMA((2 * count,)),
            pltpu.SemaphoreType.DMA((count + 1,)),
        ],
        compiler_params=BIG,
        name="join",
    )(keep, got, *extra)


def each_chunk(rows, step):
    def run(c, _):
        step(pl.ds(pl.multiple_of(c * CHUNK, CHUNK), CHUNK), c)
        return 0

    lax.fori_loop(0, rows // CHUNK, run, 0)


def total_of(refs, part):
    total = refs[0][part, :].astype(F32)
    for ref in refs[1:]:
        total = total + ref[part, :].astype(F32)
    return total


def add_kernel(*refs):
    def step(part, c):
        refs[-1][part, :] = total_of(refs[:-1], part).astype(refs[-1].dtype)

    each_chunk(refs[-1].shape[0], step)


def add(*values):
    rows, width = values[0].shape
    block = pl.BlockSpec((rows // 2, width), lambda i: (i, 0))
    return pl.pallas_call(
        add_kernel,
        grid=(2,),
        out_shape=jax.ShapeDtypeStruct((rows, width), BF16),
        in_specs=[block] * len(values),
        out_specs=block,
        compiler_params=BIG,
        name="add",
    )(*values)


def split_kernel(*refs):
    half = refs[-1].shape[0]

    def step(part, c):
        refs[-2][part, :] = total_of(refs[:-2], part)
        other = pl.ds(pl.multiple_of(half + c * CHUNK, CHUNK), CHUNK)
        refs[-1][part, :] = total_of(refs[:-2], other)

    each_chunk(half, step)


def split_total(*values):
    shape = jax.ShapeDtypeStruct((values[0].shape[0] // 2, values[0].shape[1]), F32)
    return pl.pallas_call(
        split_kernel,
        out_shape=(shape, shape),
        in_specs=[VMEM] * len(values),
        out_specs=(VMEM, VMEM),
        compiler_params=BIG,
        name="split_total",
    )(*values)


def finish_kernel(scale, image, text, kept, got, far, last, got_far, got_last, image_grad, text_grad):
    core = lax.axis_index("col") % 2

    def backward(raw, parts):
        unit, inverse = normalize(raw[...])
        unit_grad = scale[0] * (parts[0][...] + parts[1][...].astype(F32) + parts[2][...].astype(F32))
        along = jnp.sum(unit * unit_grad, axis=1, keepdims=True)
        return inverse * (unit_grad - unit * along)

    @pl.when(core == 0)
    def _():
        image_grad[...] = backward(image, (kept, far, last))
        text_grad[...] = backward(text, (got, got_far, got_last))

    @pl.when(core == 1)
    def _():
        image_grad[...] = backward(image, (got, got_far, got_last))
        text_grad[...] = backward(text, (kept, far, last))


def finish(scale, image, text, kept, got, far, last):
    rows, width = image.shape
    shape = jax.ShapeDtypeStruct(image.shape, F32)
    block = pl.BlockSpec((rows // 2, width), lambda i: (i, 0))
    other = pl.BlockSpec((rows // 2, width), lambda i: (2 + i, 0))
    return pl.pallas_call(
        finish_kernel,
        grid=(2,),
        out_shape=(shape, shape),
        in_specs=[SMEM] + [block] * 6 + [other] * 2,
        out_specs=(block, block),
        compiler_params=BIG,
        name="finish",
    )(scale, image, text, kept, got, far, last, send(far, CORES), send(last, CORES))


def after(values, first):
    return lax.optimization_barrier((tuple(values), first))


def after(values, first):
    return list(lax.optimization_barrier((tuple(values), first))[0])


def shards(image, text, labels, sharpness, shift):
    scale = (sharpness, shift)
    rows = 2 * image.shape[0]
    own0 = prepare(image, text, labels)
    mate0 = send(own0, MATES)
    up, down, far = (send(own0, ring(-d)) for d in STEPS[1:])
    own = [own0, up, down, mate0]
    own_other = [send(piece, CORES) for piece in own]
    mate = [far] + [send(mate0, ring(-d)) for d in STEPS[1:3]] + [send(far, MATES)]
    before = own_sums(scale, own, own_other)
    mate = mate[:1] + after(mate[1:], before)
    mate_other = [send(piece, CORES) for piece in mate]
    keeps, aways = rest_sums(scale, own + mate, own_other + mate_other, before)

    gone = send(aways[0], CORES)
    own_gone, last_gone = (send(away, CORES) for away in after(aways[1:], gone))
    mate_up, mate_down, far = join(keeps[0], gone, rows, (0, 1, 2))
    far = send(far, MATES)
    mate_up, mate_down = send(mate_up, ring(1)), send(mate_down, ring(-1))
    up, down = join(keeps[1], own_gone, rows, (0, 1))
    up, down = send(up, ring(1)), send(down, ring(-1))
    (far,) = join(keeps[2], last_gone, rows, (1,), (far,))
    own_part, mate_part = join(keeps[2], last_gone, rows, (0, 2))
    (mate_part,) = after((mate_part,), far)
    far = send(far, ring(2))
    mate_total = send(add(mate_part, mate_up, mate_down), MATES)
    kept, away = split_total(own_part, up, down)
    return finish(sharpness, image, text, kept, send(away, CORES), far, mate_total)


def solution(mesh):
    spec = P(AXES, None)
    return jax.shard_map(
        shards,
        mesh=mesh,
        in_specs=(spec, spec, P(AXES), P(), P()),
        out_specs=(spec, spec),
        check_vma=False,
    )
```
